32 devices in a mesh: parts: 2 (over y), row: 4 (over z), col: 2 (over x), rep: 2 (over core).
Axes of the slice: x: 2, y: 2, z: 4, core: 2. Of those that a mesh axis runs over, the one named last changes fastest.
Arguments:
- samples: float32 [192, 4096], P('parts', ('row', 'col', 'rep')), parts along dimension 0, may hold values from -6 to 6
- diag_tiles: float32 [32, 256, 256], P(('parts', 'row', 'col', 'rep')), parts along dimension 0, may hold values from -1 to 2, as said below
- omega_slots: float32 [8, 4, 8, 256, 256], P(('parts', 'row'), ('col', 'rep')), parts along dimension 0, may hold values from -1 to 1, as said below
- tile_pos: int32 [8, 4, 8, 2], P(('parts', 'row'), ('col', 'rep')), parts along dimension 0, may hold values from 0 to 3, as said below
- tile_count: int32 [8, 4], P(('parts', 'row'), ('col', 'rep')), parts along dimension 0, may hold values from 0 to 8, as said below
Outputs:
- new_slots: float32 [8, 4, 8, 256, 256], P(('parts', 'row'), ('col', 'rep')), parts along dimension 0
- new_diag: float32 [32, 256, 256], P(('parts', 'row', 'col', 'rep')), parts along dimension 0
The draws below stay inside these ranges and needn't reach their ends.
There are 2 independent parts, one for each index of `parts`. The reference program is written for one: setup_inputs(seed, part) draws one part's arguments, and reference() takes and returns one part's arrays. A program takes and returns all parts, laid end to end along the dimension named above; each array names one. Nothing has to cross between parts.
Inputs may be any that keep to these rules, and one draw needn't show every extreme that they name: `tile_pos`: live slots of a cell name distinct blocks. The pattern and Omega are symmetric: slot s of cell (b, a) names the transposed block of slot s of cell (a, b) and holds its tile transposed, with the same count; in a cell (a, a) the slots 2k and 2k + 1 hold a block and its transpose, never a diagonal block. `tile_count`: equal for cells (a, b) and (b, a), even for cells (a, a); some cell holds 8 in every draw. `omega_slots`: symmetric as a whole matrix together with the slots (see tile_pos). `diag_tiles`: each block is symmetric, with diagonal entries from 1 to 2.
All inputs are finite; a program needn't handle non-finite values.
Results may differ from the reference program's by a relative error of at most 0.0001.
Values sent between devices are 32-bit elements; how exact they have to be, the bound alone decides.
No kernel may reach another device: no remote copies, remote signals or barrier semaphores. Data moves between devices by JAX's collectives and lax.ppermute only.
A program may use at most 64 MiB of HBM per device.

```python
import jax
import jax.numpy as jnp
from jax import lax

TILE = 256
SAMPLES = 96
SLOTS = 8
GROUPS = 4
BLOCKS = 16
VOXELS = 4096


def tile_pattern(key):
    span_size = GROUPS
    weights = jax.random.randint(jax.random.fold_in(key, 11), (span_size,), 1, 5)
    hottest = jax.random.randint(jax.random.fold_in(key, 12), (), 0, span_size)
    grid_line = jnp.arange(span_size)
    weights = jnp.where(grid_line == hottest, 4, weights)
    extra_one = jax.random.randint(jax.random.fold_in(key, 13), (span_size, span_size), 0, 2)
    upper_half = grid_line[:, None] <= grid_line[None, :]
    extra_one = jnp.where(upper_half, extra_one, extra_one.T)
    counts = jnp.minimum(SLOTS, weights[:, None] * weights[None, :] * SLOTS // 16 + extra_one)
    diagonal = grid_line[:, None] == grid_line[None, :]
    counts = jnp.where(diagonal, counts - counts % 2, counts)
    cells = span_size * span_size
    cell_keys = jax.random.split(jax.random.fold_in(key, 14), cells)

    def order_cells(one_key):
        return jax.random.permutation(one_key, cells)
    orders = jax.vmap(order_cells)(cell_keys)
    grid_row = grid_line[:, None]
    grid_col = grid_line[None, :]
    canonical = jnp.minimum(grid_row, grid_col) * span_size + jnp.maximum(grid_row, grid_col)
    chosen = orders[canonical][:, :, :SLOTS]
    first_index = chosen // span_size
    second_index = chosen % span_size
    swapped = (grid_row > grid_col)[:, :, None]
    place_row = jnp.where(swapped, second_index, first_index)
    place_col = jnp.where(swapped, first_index, second_index)
    pairs_row, pairs_col = jnp.triu_indices(span_size, 1)
    pair_total = span_size * (span_size - 1) // 2
    pair_keys = jax.random.split(jax.random.fold_in(key, 15), span_size)

    def order_pairs(one_key):
        return jax.random.permutation(one_key, pair_total)
    pair_orders = jax.vmap(order_pairs)(pair_keys)
    slot_line = jnp.arange(SLOTS)
    pair_index = slot_line // 2
    odd_slot = (slot_line % 2 == 1)[None, :]
    picked = pair_orders[:, pair_index]
    diag_row = jnp.where(odd_slot, pairs_col[picked], pairs_row[picked])
    diag_col = jnp.where(odd_slot, pairs_row[picked], pairs_col[picked])
    on_diag = diagonal[:, :, None]
    place_row = jnp.where(on_diag, diag_row[:, None, :], place_row)
    place_col = jnp.where(on_diag, diag_col[:, None, :], place_col)
    places = jnp.stack([place_row, place_col], axis=-1).astype(jnp.int32)
    return (counts.astype(jnp.int32), places)


def draw_tile_count(key, part):
    counts, places = tile_pattern(key)
    return counts


def draw_tile_pos(key, part):
    counts, places = tile_pattern(key)
    return places


def draw_omega_slots(key, part):
    key = jax.random.fold_in(key, 3)
    shape_all = (GROUPS, GROUPS, SLOTS, TILE, TILE)
    raw_tiles = jax.random.normal(key, shape_all, jnp.float32) * 0.1
    mirror = jnp.swapaxes(jnp.swapaxes(raw_tiles, 0, 1), 3, 4)
    slot_line = jnp.arange(SLOTS)
    even_source = raw_tiles[:, :, slot_line // 2 * 2]
    odd_slot = (slot_line % 2 == 1)[None, None, :, None, None]
    diag_values = jnp.where(odd_slot, jnp.swapaxes(even_source, 3, 4), even_source)
    grid_line = jnp.arange(GROUPS)
    below = (grid_line[:, None] < grid_line[None, :])[:, :, None, None, None]
    above = (grid_line[:, None] > grid_line[None, :])[:, :, None, None, None]
    return jnp.where(below, raw_tiles, jnp.where(above, mirror, diag_values))


def draw_diag_tiles(key, part):
    key = jax.random.fold_in(key, 4)
    shape_all = (BLOCKS, TILE, TILE)
    raw_tiles = jax.random.normal(key, shape_all, jnp.float32) * 0.1
    symmetric = (raw_tiles + jnp.swapaxes(raw_tiles, 1, 2)) * 0.5
    diag_entries = jax.random.uniform(jax.random.fold_in(key, 5), (BLOCKS, TILE), jnp.float32, 1.0, 2.0)
    identity = jnp.eye(TILE, dtype=jnp.float32)[None]
    return symmetric * (1.0 - identity) + identity * diag_entries[:, None, :]


def shard_levels(key, extent, cuts, least, high):
    def one(position, parts):
        steps = jax.random.uniform(jax.random.fold_in(jax.random.fold_in(key, 6), position), (parts,), jnp.float32, least / len(cuts), high / len(cuts))
        return jnp.repeat(jnp.exp(steps), extent[position] // parts).reshape((-1,) + (1,) * (len(extent) - position - 1))

    loudness = one(*cuts[0])
    for cut in cuts[1:]:
        loudness = loudness * one(*cut)
    return loudness


def gaussian(stream_key, dims, scale, bound, cuts=(), kind=jnp.bfloat16):
    level = shard_levels(stream_key, dims, cuts, -0.22, 0.18) if cuts else 1.0
    values = jax.random.normal(stream_key, dims, jnp.float32) * scale * level
    return jnp.minimum(jnp.maximum(values, -bound), bound).astype(kind)


def setup_inputs(seed: int = 0, part: int = 0) -> dict:
    arg_keys = jax.random.split(jax.random.key(seed), 6)
    part_keys = jax.random.split(jax.random.fold_in(arg_keys[5], part), 6)
    return {
        "samples": gaussian(part_keys[0], (SAMPLES, VOXELS), 1.0, 6.0, ((1, 16),), jnp.float32),
        "diag_tiles": draw_diag_tiles(jax.random.fold_in(jax.random.fold_in(arg_keys[5], part), 71), part),
        "omega_slots": draw_omega_slots(jax.random.fold_in(jax.random.fold_in(arg_keys[5], part), 71), part),
        "tile_pos": draw_tile_pos(jax.random.fold_in(jax.random.fold_in(arg_keys[5], part), 71), part),
        "tile_count": draw_tile_count(jax.random.fold_in(jax.random.fold_in(arg_keys[5], part), 71), part),
    }


highest = lax.Precision.HIGHEST
step_size = 1.0
penalty = 0.1


def soft_limit(values):
    limit_value = step_size * penalty
    return values - jnp.clip(values, -limit_value, limit_value)


def product(left, right):
    return jnp.dot(left, right, precision=highest, preferred_element_type=jnp.float32)


def reference(samples, diag_tiles, omega_slots, tile_pos, tile_count):
    blocks = jnp.moveaxis(samples.reshape(SAMPLES, BLOCKS, TILE), 1, 0)
    grid_index = jnp.arange(GROUPS).astype(jnp.int32)
    row_block = (grid_index[:, None, None] * GROUPS + tile_pos[:, :, :, 0]).astype(jnp.int32).reshape(-1)
    col_block = (grid_index[None, :, None] * GROUPS + tile_pos[:, :, :, 1]).astype(jnp.int32).reshape(-1)
    slot_ids = jnp.arange(SLOTS).astype(jnp.int32)
    alive = (slot_ids[None, None, :] < tile_count[:, :, None]).astype(jnp.float32).reshape(-1)
    flat_tiles = omega_slots.reshape(GROUPS * GROUPS * SLOTS, TILE, TILE)
    image = jnp.einsum('bnk,bkt->bnt', blocks, diag_tiles, precision=highest)

    def add_slot(running, slot_item):
        target, source_index, weight, slot_tile = slot_item
        source = lax.dynamic_index_in_dim(blocks, source_index, 0, keepdims=False)
        slot_term = product(source, slot_tile.T) * weight
        current = lax.dynamic_index_in_dim(running, target, 0, keepdims=False)
        return lax.dynamic_update_index_in_dim(running, current + slot_term, target, 0), None

    image, _ = lax.scan(add_slot, image, (row_block, col_block, alive, flat_tiles))

    def update_slot(slot_item):
        target, source_index, weight, slot_tile = slot_item
        panel_row = lax.dynamic_index_in_dim(blocks, target, 0, keepdims=False)
        panel_col = lax.dynamic_index_in_dim(blocks, source_index, 0, keepdims=False)
        image_row = lax.dynamic_index_in_dim(image, target, 0, keepdims=False)
        image_col = lax.dynamic_index_in_dim(image, source_index, 0, keepdims=False)
        gradient = (product(panel_row.T, image_col) + product(image_row.T, panel_col)) / (2.0 * SAMPLES)
        return soft_limit(slot_tile - step_size * gradient) * weight

    new_slots = lax.map(update_slot, (row_block, col_block, alive, flat_tiles)).reshape(omega_slots.shape)

    def update_diag(diag_item):
        panel_own, image_own, slot_tile = diag_item
        identity = jnp.eye(TILE, dtype=jnp.float32)
        gradient = (product(panel_own.T, image_own) + product(image_own.T, panel_own)) / (2.0 * SAMPLES)
        gradient = gradient - identity / jnp.diagonal(slot_tile)[None, :]
        shifted = slot_tile - step_size * gradient
        return identity * shifted + (1.0 - identity) * soft_limit(shifted)

    new_diag = lax.map(update_diag, (blocks, image, diag_tiles))
    return new_slots, new_diag
```

```python
import functools

import jax
import jax.numpy as jnp
from jax import lax
from jax.experimental import pallas as pl
from jax.experimental.pallas import tpu as pltpu
from jax.sharding import PartitionSpec as P

step_size = 1.0
penalty = 0.1
grid_axes = ("row", "col", "rep")
line_axes = ("col", "rep")
f32 = jnp.float32
bf16 = jnp.bfloat16
vmem = pl.BlockSpec(memory_space=pltpu.VMEM)
smem = pl.BlockSpec(memory_space=pltpu.SMEM)


def halves(values):
    high = values.astype(bf16)
    return high, (values - high.astype(f32)).astype(bf16)


def dot(left, right, dims):
    return lax.dot_general(left, right, (dims, ((), ())), preferred_element_type=f32)


def soft_limit(values):
    limit_value = step_size * penalty
    return values - jnp.clip(values, -limit_value, limit_value)


def split_kernel(tiles, high, low):
    high[...], low[...] = halves(tiles[...])


def split_tiles(tiles):
    slots, side, _ = tiles.shape
    block = pl.BlockSpec((1, side, side), lambda s: (s, 0, 0))
    shape = jax.ShapeDtypeStruct(tiles.shape, bf16)
    return pl.pallas_call(
        split_kernel,
        grid=(slots,),
        out_shape=(shape, shape),
        in_specs=[block],
        out_specs=(block, block),
        name="split_tiles",
    )(tiles)


def partial_kernel(groups, place, count, samples, diag, high, low, *refs):
    pieces = refs[:groups]
    kept, sent, panel, total = refs[groups:]
    row = lax.axis_index("row")
    col = lax.axis_index("col")
    rep = lax.axis_index("rep")
    rows = samples.shape[0]
    for turn in range(groups):
        block = lax.rem(row + turn, groups)
        panel[block, :rows], panel[block, rows:] = halves(pieces[turn][...])
    total[...] = jnp.zeros_like(total)

    def term(x_high, both, w_high, w_low, dims):
        wide = dot(both, w_high, dims)
        return wide[:rows] + wide[rows:] + dot(x_high, w_low, dims)

    own_high, own_low = halves(samples[...])
    total[col * 2 + rep] = term(
        own_high, jnp.concatenate([own_high, own_low], axis=0), *halves(diag[0]), ((1,), (0,))
    )
    for slot in range(high.shape[0]):

        @pl.when(slot < count[0, 0])
        def _():
            source = panel.at[place[slot, 1]]
            total[place[slot, 0]] += term(
                source[:rows], source[...], high[slot], low[slot], ((1,), (1,))
            )

    for pair in range(groups // 2):
        kept[pair] = total[2 * pair + rep]
        sent[pair] = total[2 * pair + 1 - rep]


def partial_image(place, count, samples, diag, high, low, pieces):
    groups = len(pieces)
    rows, side = samples.shape
    shape = jax.ShapeDtypeStruct((groups // 2, rows, side), f32)
    return pl.pallas_call(
        functools.partial(partial_kernel, groups),
        out_shape=(shape, shape),
        in_specs=[smem, smem] + [vmem] * (4 + groups),
        out_specs=(vmem, vmem),
        scratch_shapes=[
            pltpu.VMEM((groups, 2 * rows, side), bf16),
            pltpu.VMEM((groups, rows, side), f32),
        ],
        compiler_params=pltpu.CompilerParams(vmem_limit_bytes=48 * 2**20),
        name="partial_image",
    )(place, count, samples, diag, high, low, *pieces)


def panels_kernel(groups, own_image, other_image, *refs):
    row_pieces, col_pieces = refs[:groups], refs[groups : 2 * groups]
    left_high, left_low, right_high, right_low = refs[2 * groups :]
    row = lax.axis_index("row")
    own = lax.axis_index("col") * 2 + lax.axis_index("rep")
    rep = lax.axis_index("rep")
    rows = own_image.shape[1]
    for turn in range(groups):
        block = lax.rem(own + groups - turn, groups)
        high, low = halves(row_pieces[turn][...].T)
        left_high[block, :, :rows], left_low[block, :, :rows] = high, low
        block = lax.rem(row + turn, groups)
        right_high[block], right_low[block] = halves(col_pieces[turn][...])
    for pair in range(groups // 2):
        for parity, image in ((rep, own_image), (1 - rep, other_image)):
            high, low = halves(image[pair].T)
            block = 2 * pair + parity
            left_high[block, :, rows:], left_low[block, :, rows:] = high, low


def early_panels(own_image, other_image, row_pieces, col_pieces):
    groups = len(row_pieces)
    _, rows, side = own_image.shape
    left = jax.ShapeDtypeStruct((groups, side, 2 * rows), bf16)
    right = jax.ShapeDtypeStruct((groups, rows, side), bf16)
    return pl.pallas_call(
        functools.partial(panels_kernel, groups),
        out_shape=(left, left, right, right),
        in_specs=[vmem] * (2 + 2 * groups),
        out_specs=(vmem,) * 4,
        compiler_params=pltpu.CompilerParams(vmem_limit_bytes=48 * 2**20),
        name="early_panels",
    )(own_image, other_image, *row_pieces, *col_pieces)


def slots_kernel(
    groups, place, count, left_high, left_low, x_high, x_low, first, second, tiles, out, high, low
):
    slot = pl.program_id(0)
    half = groups // 2
    rows = x_high.shape[1]

    @pl.when(slot == 0)
    def _():
        turned = lax.div(lax.axis_index("row"), half)
        for pair in range(half):
            for turn, piece in enumerate((first, second)):
                block = 2 * pair + lax.rem(turned + turn, 2)
                high[block, :rows], low[block, :rows] = halves(piece[pair])
        for block in range(groups):
            high[block, rows:] = x_high[block]
            low[block, rows:] = x_low[block]

    alive = slot < count[0, 0]

    @pl.when(alive)
    def _():
        left, right = place[slot, 0], place[slot, 1]
        dims = ((1,), (0,))
        gradient = dot(left_high[left], high[right], dims)
        gradient += dot(left_low[left], high[right], dims)
        gradient += dot(left_high[left], low[right], dims)
        out[0] = soft_limit(tiles[0] - gradient * (step_size / (2.0 * rows)))

    @pl.when(jnp.logical_not(alive))
    def _():
        out[...] = jnp.zeros_like(out)


def update_slots(place, count, left_high, left_low, x_high, x_low, first, second, tiles):
    groups, rows, side = x_high.shape
    block = pl.BlockSpec((1, side, side), lambda s: (s, 0, 0))
    return pl.pallas_call(
        functools.partial(slots_kernel, groups),
        grid=(tiles.shape[0],),
        out_shape=jax.ShapeDtypeStruct(tiles.shape, f32),
        in_specs=[smem, smem] + [vmem] * 6 + [block],
        out_specs=block,
        scratch_shapes=[pltpu.VMEM((groups, 2 * rows, side), bf16)] * 2,
        compiler_params=pltpu.CompilerParams(vmem_limit_bytes=48 * 2**20),
        name="update_slots",
    )(place, count, left_high, left_low, x_high, x_low, first, second, tiles)


def diag_kernel(samples, image, tiles, out):
    rows, side = samples.shape
    own = image[lax.axis_index("col")]
    left_high, left_low = halves(samples[...].T)
    right_high, right_low = halves(own)
    dims = ((1,), (0,))
    one_side = dot(left_high, right_high, dims) + dot(left_low, right_high, dims)
    one_side += dot(left_high, right_low, dims)
    tile = tiles[0]
    row = lax.broadcasted_iota(jnp.int32, (side, side), 0)
    on_diag = row == lax.broadcasted_iota(jnp.int32, (side, side), 1)
    gradient = (one_side + one_side.T) * (1.0 / (2.0 * rows))
    shifted = tile - step_size * gradient
    inverse = step_size / jnp.where(on_diag, tile, 1.0)
    out[0] = jnp.where(on_diag, shifted + inverse, soft_limit(shifted))


def update_diag(samples, image, tiles):
    return pl.pallas_call(
        diag_kernel,
        out_shape=jax.ShapeDtypeStruct(tiles.shape, f32),
        in_specs=[vmem] * 3,
        out_specs=vmem,
        name="update_diag",
    )(samples, image, tiles)


def on_device(samples, diag_tiles, omega_slots, tile_pos, tile_count):
    groups = lax.axis_size(line_axes)
    cols = lax.axis_size("col")
    slots, side = omega_slots.shape[2], omega_slots.shape[3]
    tiles = omega_slots.reshape(slots, side, side)
    place = tile_pos.reshape(slots, 2)
    span = range(groups)

    def from_row_line(turn):
        return [
            (line * groups + j, (j - turn) % groups * groups + line) for line in span for j in span
        ]

    def around(size, turn):
        return [(j, (j + turn) % size) for j in range(size)]

    col_pieces = [lax.ppermute(samples, grid_axes, from_row_line(turn)) for turn in span]
    row_pieces = [samples] + [
        lax.ppermute(samples, line_axes, around(groups, turn)) for turn in span[1:]
    ]
    high, low = split_tiles(tiles)
    kept, sent = partial_image(place, tile_count, samples, diag_tiles, high, low, col_pieces)
    chip = kept + lax.ppermute(sent, "rep", around(2, 1))
    image = chip
    for turn in range(1, cols):
        image = image + lax.ppermute(chip, "col", around(cols, turn))

    def to_row(turn):
        return [
            (line * groups + x * 2 + r, ((r + turn) % 2 * cols + x) * groups + line)
            for line in span
            for x in range(cols)
            for r in range(2)
        ]

    first, second = [lax.ppermute(image, grid_axes, to_row(turn)) for turn in range(2)]
    other = lax.ppermute(image, "rep", around(2, 1))
    panels = early_panels(image, other, row_pieces, col_pieces)
    new_diag = update_diag(samples, image, diag_tiles)
    new_slots = update_slots(place, tile_count, *panels, first, second, tiles)
    return new_slots.reshape(omega_slots.shape), new_diag


def solution(mesh):
    placed = (
        P("parts", ("row", "col", "rep")),
        P(("parts", "row", "col", "rep"), None, None),
        P(("parts", "row"), ("col", "rep"), None, None, None),
        P(("parts", "row"), ("col", "rep"), None, None),
        P(("parts", "row"), ("col", "rep")),
    )
    return jax.shard_map(
        on_device,
        mesh=mesh,
        in_specs=placed,
        out_specs=(
            P(("parts", "row"), ("col", "rep"), None, None, None),
            P(("parts", "row", "col", "rep"), None, None),
        ),
        check_vma=False,
    )
```

```python
import functools

import jax
import jax.numpy as jnp
from jax import lax
from jax.experimental import pallas as pl
from jax.experimental.pallas import tpu as pltpu
from jax.sharding import PartitionSpec as P

step_size = 1.0
penalty = 0.1
grid_axes = ("row", "col", "rep")
line_axes = ("col", "rep")
f32 = jnp.float32
bf16 = jnp.bfloat16
vmem = pl.BlockSpec(memory_space=pltpu.VMEM)
smem = pl.BlockSpec(memory_space=pltpu.SMEM)
room = pltpu.CompilerParams(vmem_limit_bytes=24 * 2**20)


def halves(values):
    high = values.astype(bf16)
    return high, (values - high.astype(f32)).astype(bf16)


def dot(left, right, dims):
    return lax.dot_general(left, right, (dims, ((), ())), preferred_element_type=f32)


def soft_limit(values):
    limit_value = step_size * penalty
    return values - jnp.clip(values, -limit_value, limit_value)


def prepare_kernel(groups, tiles, *refs):
    pieces = refs[:groups]
    high, low, left_high, left_low = refs[groups:]
    own = lax.axis_index("col") * 2 + lax.axis_index("rep")
    for slot in range(tiles.shape[0]):
        high[slot], low[slot] = halves(tiles[slot])
    for turn in range(groups):
        block = lax.rem(own + groups - turn, groups)
        left_high[block], left_low[block] = halves(pieces[turn][...].T)


def prepare(tiles, pieces):
    groups = len(pieces)
    rows, side = pieces[0].shape
    tile = jax.ShapeDtypeStruct(tiles.shape, bf16)
    left = jax.ShapeDtypeStruct((groups, side, rows), bf16)
    return pl.pallas_call(
        functools.partial(prepare_kernel, groups),
        out_shape=(tile, tile, left, left),
        in_specs=[vmem] * (1 + groups),
        out_specs=(vmem,) * 4,
        compiler_params=room,
        name="prepare",
    )(tiles, *pieces)


def partial_kernel(groups, place, count, samples, diag, high, low, *refs):
    pieces = refs[:groups]
    kept, sent, panel, total = refs[groups:]
    row = lax.axis_index("row")
    col = lax.axis_index("col")
    rep = lax.axis_index("rep")
    rows = samples.shape[0]
    for turn in range(groups):
        block = lax.rem(row + turn, groups)
        panel[block, :rows], panel[block, rows:] = halves(pieces[turn][...])
    total[...] = jnp.zeros_like(total)

    def term(x_high, both, w_high, w_low, dims):
        wide = dot(both, w_high, dims)
        return wide[:rows] + wide[rows:] + dot(x_high, w_low, dims)

    own_high, own_low = halves(samples[...])
    total[col * 2 + rep] = term(
        own_high, jnp.concatenate([own_high, own_low], axis=0), *halves(diag[0]), ((1,), (0,))
    )
    for slot in range(high.shape[0]):
        source = panel.at[place[1, slot]]
        value = term(source[:rows], source[...], high[slot], low[slot], ((1,), (1,)))
        total[place[0, slot]] += jnp.where(slot < count[0, 0], value, 0.0)
    for pair in range(groups // 2):
        kept[pair] = total[2 * pair + rep]
        sent[pair] = total[2 * pair + 1 - rep]


def partial_image(place, count, samples, diag, high, low, pieces):
    groups = len(pieces)
    rows, side = samples.shape
    shape = jax.ShapeDtypeStruct((groups // 2, rows, side), f32)
    panel = jax.ShapeDtypeStruct((groups, 2 * rows, side), bf16)
    return pl.pallas_call(
        functools.partial(partial_kernel, groups),
        out_shape=(shape, shape, panel),
        in_specs=[smem, smem] + [vmem] * (4 + groups),
        out_specs=(vmem, vmem, vmem),
        scratch_shapes=[pltpu.VMEM((groups, rows, side), f32)],
        compiler_params=room,
        name="partial_image",
    )(place, count, samples, diag, high, low, *pieces)


def left_kernel(own_image, other_image, x_high, x_low, high, low):
    rep = lax.axis_index("rep")
    rows = own_image.shape[1]
    half = high.shape[2] // 2
    for block in range(high.shape[0]):
        for out, part in ((high, x_high), (low, x_low)):
            out[block] = jnp.zeros(out.shape[1:], bf16)
            out[block, :, :rows] = part[block]
    for pair in range(own_image.shape[0]):
        for parity, image in ((rep, own_image), (1 - rep, other_image)):
            block = 2 * pair + parity
            image_high, image_low = halves(image[pair].T)
            high[block, :, half : half + rows] = image_high
            low[block, :, half : half + rows] = image_low


def left_panels(own_image, other_image, x_high, x_low):
    groups, side, rows = x_high.shape
    depth = 2 * -(-rows // 128) * 128
    left = jax.ShapeDtypeStruct((groups, side, depth), bf16)
    return pl.pallas_call(
        left_kernel,
        out_shape=(left, left),
        in_specs=[vmem] * 4,
        out_specs=(vmem,) * 2,
        compiler_params=room,
        name="left_panels",
    )(own_image, other_image, x_high, x_low)


def slots_kernel(
    place, count, left_high, left_low, panel, first, second, tiles, out, high, low, ready, sems
):
    groups = panel.shape[0]
    rows = panel.shape[1] // 2
    half = high.shape[1] // 2
    turned = lax.div(lax.axis_index("row"), groups // 2)
    for ref in (high, low):
        for start in (rows, half + rows):
            blank = jnp.zeros((groups, half - rows, high.shape[2]), bf16)
            ref[:, start : start + half - rows] = blank
    for pair in range(groups // 2):
        for turn, piece in enumerate((first, second)):
            block = 2 * pair + lax.rem(turned + turn, 2)
            high[block, :rows], low[block, :rows] = halves(piece[pair])
    high[:, half : half + rows] = panel[:, :rows]
    low[:, half : half + rows] = panel[:, rows:]
    dims = ((1,), (0,))
    copies = []
    for slot in range(tiles.shape[0]):
        left, right = place[0, slot], place[1, slot]
        gradient = dot(left_high[left], high[right], dims)
        gradient += dot(left_low[left], high[right], dims)
        gradient += dot(left_high[left], low[right], dims)
        value = soft_limit(tiles[slot] - gradient * (step_size / (2.0 * rows)))
        ready[slot] = jnp.where(slot < count[0, 0], value, 0.0)
        copies.append(pltpu.make_async_copy(ready.at[slot], out.at[slot], sems.at[slot]))
        copies[-1].start()
    for copy in copies:
        copy.wait()


def update_slots(place, count, left_high, left_low, panel, first, second, tiles):
    slots, side, _ = tiles.shape
    groups, _, depth = left_high.shape
    return pl.pallas_call(
        slots_kernel,
        out_shape=jax.ShapeDtypeStruct(tiles.shape, f32),
        in_specs=[smem, smem] + [vmem] * 6,
        out_specs=pl.BlockSpec(memory_space=pl.ANY),
        scratch_shapes=[
            pltpu.VMEM((groups, depth, side), bf16),
            pltpu.VMEM((groups, depth, side), bf16),
            pltpu.VMEM(tiles.shape, f32),
            pltpu.SemaphoreType.DMA((slots,)),
        ],
        compiler_params=room,
        name="update_slots",
    )(place, count, left_high, left_low, panel, first, second, tiles)


def diag_kernel(samples, image, tiles, out):
    rows, side = samples.shape
    own = image[lax.axis_index("col")]
    left_high, left_low = halves(samples[...].T)
    right_high, right_low = halves(own)
    dims = ((1,), (0,))
    one_side = dot(left_high, right_high, dims) + dot(left_low, right_high, dims)
    one_side += dot(left_high, right_low, dims)
    tile = tiles[0]
    row = lax.broadcasted_iota(jnp.int32, (side, side), 0)
    on_diag = row == lax.broadcasted_iota(jnp.int32, (side, side), 1)
    gradient = (one_side + one_side.T) * (1.0 / (2.0 * rows))
    shifted = tile - step_size * gradient
    inverse = step_size / jnp.where(on_diag, tile, 1.0)
    out[0] = jnp.where(on_diag, shifted + inverse, soft_limit(shifted))


def update_diag(samples, image, tiles):
    return pl.pallas_call(
        diag_kernel,
        out_shape=jax.ShapeDtypeStruct(tiles.shape, f32),
        in_specs=[vmem] * 3,
        out_specs=vmem,
        name="update_diag",
    )(samples, image, tiles)


def on_device(samples, diag_tiles, omega_slots, tile_pos, tile_count):
    groups = lax.axis_size(line_axes)
    cols = lax.axis_size("col")
    slots, side = omega_slots.shape[2], omega_slots.shape[3]
    tiles = omega_slots.reshape(slots, side, side)
    place = tile_pos.reshape(slots, 2).T
    span = range(groups)

    def from_row_line(turn):
        return [
            (line * groups + j, (j - turn) % groups * groups + line) for line in span for j in span
        ]

    def around(size, turn):
        return [(j, (j + turn) % size) for j in range(size)]

    col_pieces = [lax.ppermute(samples, grid_axes, from_row_line(turn)) for turn in span]
    row_pieces = [samples] + [
        lax.ppermute(samples, line_axes, around(groups, turn)) for turn in span[1:]
    ]
    high, low, *left_x = prepare(tiles, row_pieces)
    kept, sent, panel = partial_image(
        place, tile_count, samples, diag_tiles, high, low, col_pieces
    )
    chip = kept + lax.ppermute(sent, "rep", around(2, 1))
    image = chip
    for turn in range(1, cols):
        image = image + lax.ppermute(chip, "col", around(cols, turn))

    def to_row(turn):
        return [
            (line * groups + x * 2 + r, ((r + turn) % 2 * cols + x) * groups + line)
            for line in span
            for x in range(cols)
            for r in range(2)
        ]

    first, second = [lax.ppermute(image, grid_axes, to_row(turn)) for turn in range(2)]
    other = lax.ppermute(image, "rep", around(2, 1))
    left = left_panels(image, other, *left_x)
    new_diag = update_diag(samples, image, diag_tiles)
    new_slots = update_slots(place, tile_count, *left, panel, first, second, tiles)
    return new_slots.reshape(omega_slots.shape), new_diag


def solution(mesh):
    placed = (
        P("parts", ("row", "col", "rep")),
        P(("parts", "row", "col", "rep"), None, None),
        P(("parts", "row"), ("col", "rep"), None, None, None),
        P(("parts", "row"), ("col", "rep"), None, None),
        P(("parts", "row"), ("col", "rep")),
    )
    return jax.shard_map(
        on_device,
        mesh=mesh,
        in_specs=placed,
        out_specs=(
            P(("parts", "row"), ("col", "rep"), None, None, None),
            P(("parts", "row", "col", "rep"), None, None),
        ),
        check_vma=False,
    )
```

```python
import functools

import jax
import jax.numpy as jnp
from jax import lax
from jax.experimental import pallas as pl
from jax.experimental.pallas import tpu as pltpu
from jax.sharding import PartitionSpec as P

step_size = 1.0
penalty = 0.1
grid_axes = ("row", "col", "rep")
line_axes = ("col", "rep")
f32 = jnp.float32
bf16 = jnp.bfloat16
vmem = pl.BlockSpec(memory_space=pltpu.VMEM)
smem = pl.BlockSpec(memory_space=pltpu.SMEM)
hbm = pl.BlockSpec(memory_space=pltpu.HBM)
room = pltpu.CompilerParams(vmem_limit_bytes=24 * 2**20)


def halves(values):
    high = values.astype(bf16)
    return high, (values - high.astype(f32)).astype(bf16)


def dot(left, right, dims):
    return lax.dot_general(left, right, (dims, ((), ())), preferred_element_type=f32)


def soft_limit(values):
    limit_value = step_size * penalty
    return values - jnp.clip(values, -limit_value, limit_value)


def prepare_kernel(samples, diag, tiles, own, own_diag, held, high, low, sems):
    slots = tiles.shape[0]
    copies = [
        pltpu.make_async_copy(tiles.at[slot], held.at[slot], sems.at[slot])
        for slot in range(slots)
    ]
    copies.append(pltpu.make_async_copy(samples, own, sems.at[slots]))
    copies.append(pltpu.make_async_copy(diag, own_diag, sems.at[slots + 1]))
    for copy in copies:
        copy.start()
    for slot in range(slots):
        copies[slot].wait()
        high[slot], low[slot] = halves(held[slot])
    copies[slots].wait()
    copies[slots + 1].wait()


def prepare(samples, diag, tiles):
    held = [jax.ShapeDtypeStruct(x.shape, f32) for x in (samples, diag, tiles)]
    half = jax.ShapeDtypeStruct(tiles.shape, bf16)
    return pl.pallas_call(
        prepare_kernel,
        out_shape=(*held, half, half),
        in_specs=[hbm] * 3,
        out_specs=(vmem,) * 5,
        scratch_shapes=[pltpu.SemaphoreType.DMA((tiles.shape[0] + 2,))],
        compiler_params=room,
        name="prepare",
    )(samples, diag, tiles)


def partial_kernel(groups, place, count, samples, diag, high, low, *refs):
    pieces = refs[:groups]
    beside = refs[groups:-4]
    kept, sent, panel, total = refs[-4:]
    row = lax.axis_index("row")
    col = lax.axis_index("col")
    rep = lax.axis_index("rep")
    rows = samples.shape[0]
    for turn in range(groups):
        block = lax.rem(row + turn, groups)
        panel[block, :rows], panel[block, rows:] = halves(pieces[turn][...])
    total[...] = jnp.zeros_like(total)

    def term(x_high, both, w_high, w_low, dims):
        wide = dot(both, w_high, dims)
        return wide[:rows] + wide[rows:] + dot(x_high, w_low, dims)

    own_high, own_low = halves(samples[...])
    total[col * 2 + rep] = term(
        own_high, jnp.concatenate([own_high, own_low], axis=0), *halves(diag[0]), ((1,), (0,))
    )
    for slot in range(high.shape[0]):
        source = panel.at[place[1, slot]]
        value = term(source[:rows], source[...], high[slot], low[slot], ((1,), (1,)))
        total[place[0, slot]] += jnp.where(slot < count[0, 0], value, 0.0)
    for pair in range(groups // 2):
        kept[pair] = total[2 * pair + rep]
        sent[pair] = total[2 * pair + 1 - rep]
    for turn, piece in enumerate((samples, *beside)):
        sent[groups // 2 + turn] = piece[...]


def partial_image(place, count, samples, diag, high, low, pieces, beside):
    groups = len(pieces)
    rows, side = samples.shape
    kept = jax.ShapeDtypeStruct((groups // 2, rows, side), f32)
    sent = jax.ShapeDtypeStruct((groups, rows, side), f32)
    panel = jax.ShapeDtypeStruct((groups, 2 * rows, side), bf16)
    return pl.pallas_call(
        functools.partial(partial_kernel, groups),
        out_shape=(kept, sent, panel),
        in_specs=[smem, smem] + [vmem] * (3 + groups + groups // 2),
        out_specs=(vmem, vmem, vmem),
        scratch_shapes=[pltpu.VMEM((groups, rows, side), f32)],
        compiler_params=room,
        name="partial_image",
    )(place, count, samples, diag, high, low, *pieces, *beside)


def middle_kernel(own_image, other_image, samples, diag, swapped, *refs):
    beside = refs[:-5]
    high, low, new_diag, shifted, sem = refs[-5:]
    pairs = own_image.shape[0]
    rep = lax.axis_index("rep")
    col = lax.axis_index("col")
    rows, side = samples.shape
    half = high.shape[2] // 2
    blank = jnp.zeros((side, half - rows), bf16)
    for turn, piece in enumerate((samples, *beside)):
        line = 2 * lax.rem(col + pairs - turn, pairs)
        for block, values in ((line + rep, piece[...]), (line + 1 - rep, swapped[pairs + turn])):
            for ref, part in zip((high, low), halves(values.T)):
                ref[block, :, :rows] = part
                ref[block, :, rows:half] = blank
                ref[block, :, half + rows :] = blank
    left_high, left_low = halves(samples[...].T)
    right_high, right_low = halves(own_image[col])
    dims = ((1,), (0,))
    one_side = dot(left_high, right_high, dims) + dot(left_low, right_high, dims)
    one_side += dot(left_high, right_low, dims)
    tile = diag[0]
    line = lax.broadcasted_iota(jnp.int32, (side, side), 0)
    on_diag = line == lax.broadcasted_iota(jnp.int32, (side, side), 1)
    gradient = (one_side + one_side.T) * (1.0 / (2.0 * rows))
    moved = tile - step_size * gradient
    inverse = step_size / jnp.where(on_diag, tile, 1.0)
    shifted[0] = jnp.where(on_diag, moved + inverse, soft_limit(moved))
    copy = pltpu.make_async_copy(shifted, new_diag, sem)
    copy.start()
    for pair in range(pairs):
        for parity, image in ((rep, own_image), (1 - rep, other_image)):
            block = 2 * pair + parity
            image_high, image_low = halves(image[pair].T)
            high[block, :, half : half + rows] = image_high
            low[block, :, half : half + rows] = image_low
    copy.wait()


def middle(own_image, other_image, samples, diag, swapped, beside):
    groups = swapped.shape[0]
    rows, side = samples.shape
    depth = 2 * -(-rows // 128) * 128
    left = jax.ShapeDtypeStruct((groups, side, depth), bf16)
    return pl.pallas_call(
        middle_kernel,
        out_shape=(left, left, jax.ShapeDtypeStruct(diag.shape, f32)),
        in_specs=[vmem] * (5 + len(beside)),
        out_specs=(vmem, vmem, hbm),
        scratch_shapes=[pltpu.VMEM(diag.shape, f32), pltpu.SemaphoreType.DMA],
        compiler_params=room,
        name="middle",
    )(own_image, other_image, samples, diag, swapped, *beside)


def slots_kernel(
    place, count, left_high, left_low, panel, first, second, tiles, out, high, low, ready, sems
):
    groups = panel.shape[0]
    rows = panel.shape[1] // 2
    half = high.shape[1] // 2
    parity = lax.rem(lax.axis_index("row"), 2)
    for ref in (high, low):
        for start in (rows, half + rows):
            blank = jnp.zeros((groups, half - rows, high.shape[2]), bf16)
            ref[:, start : start + half - rows] = blank
    for pair in range(groups // 2):
        for turn, piece in enumerate((first, second)):
            block = 2 * pair + (1 - parity if turn else parity)
            high[block, :rows], low[block, :rows] = halves(piece[pair])
    high[:, half : half + rows] = panel[:, :rows]
    low[:, half : half + rows] = panel[:, rows:]
    dims = ((1,), (0,))
    copies = []
    for slot in range(tiles.shape[0]):
        left, right = place[0, slot], place[1, slot]
        gradient = dot(left_high[left], high[right], dims)
        gradient += dot(left_low[left], high[right], dims)
        gradient += dot(left_high[left], low[right], dims)
        value = soft_limit(tiles[slot] - gradient * (step_size / (2.0 * rows)))
        ready[slot] = jnp.where(slot < count[0, 0], value, 0.0)
        copies.append(pltpu.make_async_copy(ready.at[slot], out.at[slot], sems.at[slot]))
        copies[-1].start()
    for copy in copies:
        copy.wait()


def update_slots(place, count, left_high, left_low, panel, first, second, tiles):
    slots, side, _ = tiles.shape
    groups, _, depth = left_high.shape
    return pl.pallas_call(
        slots_kernel,
        out_shape=jax.ShapeDtypeStruct(tiles.shape, f32),
        in_specs=[smem, smem] + [vmem] * 6,
        out_specs=hbm,
        scratch_shapes=[
            pltpu.VMEM((groups, depth, side), bf16),
            pltpu.VMEM((groups, depth, side), bf16),
            pltpu.VMEM(tiles.shape, f32),
            pltpu.SemaphoreType.DMA((slots,)),
        ],
        compiler_params=room,
        name="update_slots",
    )(place, count, left_high, left_low, panel, first, second, tiles)


def on_device(samples, diag_tiles, omega_slots, tile_pos, tile_count):
    groups = lax.axis_size(line_axes)
    cols = lax.axis_size("col")
    slots, side = omega_slots.shape[2], omega_slots.shape[3]
    tiles = omega_slots.reshape(slots, side, side)
    place = tile_pos.reshape(slots, 2).T
    span = range(groups)

    def from_row_line(turn):
        return [
            (line * groups + j, (j - turn) % groups * groups + line) for line in span for j in span
        ]

    def around(size, turn):
        return [(j, (j + turn) % size) for j in range(size)]

    col_pieces = [lax.ppermute(samples, grid_axes, from_row_line(turn)) for turn in span]
    beside = [lax.ppermute(samples, "col", around(cols, turn)) for turn in range(1, cols)]
    own, own_diag, held, high, low = prepare(samples, diag_tiles, tiles)
    kept, sent, panel = partial_image(
        place, tile_count, own, own_diag, high, low, col_pieces, beside
    )
    swapped = lax.ppermute(sent, "rep", around(2, 1))
    chip = kept + swapped[:cols]
    image = chip
    for turn in range(1, cols):
        image = image + lax.ppermute(chip, "col", around(cols, turn))

    def to_row(turn):
        return [
            (line * groups + j, (groups - 1 - j if turn else j) * groups + line)
            for line in span
            for j in span
        ]

    first, second = [lax.ppermute(image, grid_axes, to_row(turn)) for turn in range(2)]
    other = lax.ppermute(image, "rep", around(2, 1))
    left_high, left_low, new_diag = middle(
        image, other, own, own_diag, swapped, beside
    )
    new_slots = update_slots(
        place, tile_count, left_high, left_low, panel, first, second, held
    )
    return new_slots.reshape(omega_slots.shape), new_diag


def solution(mesh):
    placed = (
        P("parts", ("row", "col", "rep")),
        P(("parts", "row", "col", "rep"), None, None),
        P(("parts", "row"), ("col", "rep"), None, None, None),
        P(("parts", "row"), ("col", "rep"), None, None),
        P(("parts", "row"), ("col", "rep")),
    )
    return jax.shard_map(
        on_device,
        mesh=mesh,
        in_specs=placed,
        out_specs=(
            P(("parts", "row"), ("col", "rep"), None, None, None),
            P(("parts", "row", "col", "rep"), None, None),
        ),
        check_vma=False,
    )
```

```python
import functools

import jax
import jax.numpy as jnp
from jax import lax
from jax.experimental import pallas as pl
from jax.experimental.pallas import tpu as pltpu
from jax.sharding import PartitionSpec as P

step_size = 1.0
penalty = 0.1
grid_axes = ("row", "col", "rep")
line_axes = ("col", "rep")
f32 = jnp.float32
bf16 = jnp.bfloat16
vmem = pl.BlockSpec(memory_space=pltpu.VMEM)
smem = pl.BlockSpec(memory_space=pltpu.SMEM)
hbm = pl.BlockSpec(memory_space=pltpu.HBM)
room = pltpu.CompilerParams(vmem_limit_bytes=24 * 2**20)


def halves(values):
    high = values.astype(bf16)
    return high, (values - high.astype(f32)).astype(bf16)


def dot(left, right, dims):
    return lax.dot_general(left, right, (dims, ((), ())), preferred_element_type=f32)


def soft_limit(values):
    limit_value = step_size * penalty
    return values - jnp.clip(values, -limit_value, limit_value)


def prepare_kernel(*refs):
    slots = refs[3].shape[0]
    sources, targets = refs[:4], refs[4:8]
    high, low, sems = refs[8:]
    tiles, held = sources[3], targets[3]
    copies = [
        pltpu.make_async_copy(tiles.at[slot], held.at[slot], sems.at[slot])
        for slot in range(slots)
    ]
    for turn in range(3):
        copies.append(pltpu.make_async_copy(sources[turn], targets[turn], sems.at[slots + turn]))
    for copy in copies:
        copy.start()
    for slot in range(slots):
        copies[slot].wait()
        high[slot], low[slot] = halves(held[slot])
    for copy in copies[slots:]:
        copy.wait()


def prepare(*arrays):
    held = [jax.ShapeDtypeStruct(x.shape, x.dtype) for x in arrays]
    half = jax.ShapeDtypeStruct(arrays[-1].shape, bf16)
    return pl.pallas_call(
        prepare_kernel,
        out_shape=(*held, half, half),
        in_specs=[hbm] * 4,
        out_specs=(smem,) + (vmem,) * 5,
        scratch_shapes=[pltpu.SemaphoreType.DMA((arrays[-1].shape[0] + 3,))],
        compiler_params=room,
        name="prepare",
    )(*[pltpu.with_memory_space_constraint(x, pltpu.HBM) for x in arrays])


def partial_kernel(groups, place, count, samples, diag, high, low, *refs):
    pieces = refs[:groups]
    beside = refs[groups:-4]
    kept, sent, panel, total = refs[-4:]
    row = lax.axis_index("row")
    col = lax.axis_index("col")
    rep = lax.axis_index("rep")
    rows = samples.shape[0]
    for turn in range(groups):
        block = lax.rem(row + turn, groups)
        panel[block, :rows], panel[block, rows:] = halves(pieces[turn][...])
    total[...] = jnp.zeros_like(total)

    def term(x_high, both, w_high, w_low, dims):
        wide = dot(both, w_high, dims)
        return wide[:rows] + wide[rows:] + dot(x_high, w_low, dims)

    own_high, own_low = halves(samples[...])
    total[col * 2 + rep] = term(
        own_high, jnp.concatenate([own_high, own_low], axis=0), *halves(diag[0]), ((1,), (0,))
    )
    for slot in range(high.shape[0]):
        source = panel.at[place[1, slot]]
        value = term(source[:rows], source[...], high[slot], low[slot], ((1,), (1,)))
        total[place[0, slot]] += jnp.where(slot < count[0, 0], value, 0.0)
    for pair in range(groups // 2):
        kept[pair] = total[2 * pair + rep]
        sent[pair] = total[2 * pair + 1 - rep]
    for turn, piece in enumerate((samples, *beside)):
        sent[groups // 2 + turn] = piece[...]


def partial_image(place, count, samples, diag, high, low, pieces, beside):
    groups = len(pieces)
    rows, side = samples.shape
    kept = jax.ShapeDtypeStruct((groups // 2, rows, side), f32)
    sent = jax.ShapeDtypeStruct((groups, rows, side), f32)
    panel = jax.ShapeDtypeStruct((groups, 2 * rows, side), bf16)
    return pl.pallas_call(
        functools.partial(partial_kernel, groups),
        out_shape=(kept, sent, panel),
        in_specs=[smem, smem] + [vmem] * (3 + groups + groups // 2),
        out_specs=(vmem, vmem, vmem),
        scratch_shapes=[pltpu.VMEM((groups, rows, side), f32)],
        compiler_params=room,
        name="partial_image",
    )(place, count, samples, diag, high, low, *pieces, *beside)


def middle_kernel(own_image, other_image, samples, diag, swapped, *refs):
    beside = refs[:-5]
    high, low, new_diag, shifted, sem = refs[-5:]
    pairs = own_image.shape[0]
    rep = lax.axis_index("rep")
    col = lax.axis_index("col")
    rows, side = samples.shape
    half = high.shape[2] // 2
    blank = jnp.zeros((side, half - rows), bf16)
    for turn, piece in enumerate((samples, *beside)):
        line = 2 * lax.rem(col + pairs - turn, pairs)
        for block, values in ((line + rep, piece[...]), (line + 1 - rep, swapped[pairs + turn])):
            for ref, part in zip((high, low), halves(values.T)):
                ref[block, :, :rows] = part
                ref[block, :, rows:half] = blank
                ref[block, :, half + rows :] = blank
    left_high, left_low = halves(samples[...].T)
    right_high, right_low = halves(own_image[col])
    dims = ((1,), (0,))
    one_side = dot(left_high, right_high, dims) + dot(left_low, right_high, dims)
    one_side += dot(left_high, right_low, dims)
    tile = diag[0]
    line = lax.broadcasted_iota(jnp.int32, (side, side), 0)
    on_diag = line == lax.broadcasted_iota(jnp.int32, (side, side), 1)
    gradient = (one_side + one_side.T) * (1.0 / (2.0 * rows))
    moved = tile - step_size * gradient
    inverse = step_size / jnp.where(on_diag, tile, 1.0)
    shifted[0] = jnp.where(on_diag, moved + inverse, soft_limit(moved))
    copy = pltpu.make_async_copy(shifted, new_diag, sem)
    copy.start()
    for pair in range(pairs):
        for parity, image in ((rep, own_image), (1 - rep, other_image)):
            block = 2 * pair + parity
            image_high, image_low = halves(image[pair].T)
            high[block, :, half : half + rows] = image_high
            low[block, :, half : half + rows] = image_low
    copy.wait()


def middle(own_image, other_image, samples, diag, swapped, beside):
    groups = swapped.shape[0]
    rows, side = samples.shape
    depth = 2 * -(-rows // 128) * 128
    left = jax.ShapeDtypeStruct((groups, side, depth), bf16)
    return pl.pallas_call(
        middle_kernel,
        out_shape=(left, left, jax.ShapeDtypeStruct(diag.shape, f32)),
        in_specs=[vmem] * (5 + len(beside)),
        out_specs=(vmem, vmem, hbm),
        scratch_shapes=[pltpu.VMEM(diag.shape, f32), pltpu.SemaphoreType.DMA],
        compiler_params=room,
        name="middle",
    )(own_image, other_image, samples, diag, swapped, *beside)


def slots_kernel(
    place, count, left_high, left_low, panel, first, second, tiles, out, high, low, ready, sems
):
    groups = panel.shape[0]
    rows = panel.shape[1] // 2
    half = high.shape[1] // 2
    parity = lax.rem(lax.axis_index("row"), 2)
    for ref in (high, low):
        for start in (rows, half + rows):
            blank = jnp.zeros((groups, half - rows, high.shape[2]), bf16)
            ref[:, start : start + half - rows] = blank
    for pair in range(groups // 2):
        for turn, piece in enumerate((first, second)):
            block = 2 * pair + (1 - parity if turn else parity)
            high[block, :rows], low[block, :rows] = halves(piece[pair])
    high[:, half : half + rows] = panel[:, :rows]
    low[:, half : half + rows] = panel[:, rows:]
    dims = ((1,), (0,))
    copies = []
    for slot in range(tiles.shape[0]):
        left, right = place[0, slot], place[1, slot]
        gradient = dot(left_high[left], high[right], dims)
        gradient += dot(left_low[left], high[right], dims)
        gradient += dot(left_high[left], low[right], dims)
        value = soft_limit(tiles[slot] - gradient * (step_size / (2.0 * rows)))
        ready[slot] = jnp.where(slot < count[0, 0], value, 0.0)
        copies.append(pltpu.make_async_copy(ready.at[slot], out.at[slot], sems.at[slot]))
        copies[-1].start()
    for copy in copies:
        copy.wait()


def update_slots(place, count, left_high, left_low, panel, first, second, tiles):
    slots, side, _ = tiles.shape
    groups, _, depth = left_high.shape
    return pl.pallas_call(
        slots_kernel,
        out_shape=jax.ShapeDtypeStruct(tiles.shape, f32),
        in_specs=[smem, smem] + [vmem] * 6,
        out_specs=hbm,
        scratch_shapes=[
            pltpu.VMEM((groups, depth, side), bf16),
            pltpu.VMEM((groups, depth, side), bf16),
            pltpu.VMEM(tiles.shape, f32),
            pltpu.SemaphoreType.DMA((slots,)),
        ],
        compiler_params=room,
        name="update_slots",
    )(place, count, left_high, left_low, panel, first, second, tiles)


def on_device(samples, diag_tiles, omega_slots, tile_pos, tile_count):
    groups = lax.axis_size(line_axes)
    cols = lax.axis_size("col")
    slots, side = omega_slots.shape[2], omega_slots.shape[3]
    tiles = omega_slots.reshape(slots, side, side)
    place = tile_pos.reshape(slots, 2).T
    span = range(groups)

    def from_row_line(turn):
        return [
            (line * groups + j, (j - turn) % groups * groups + line) for line in span for j in span
        ]

    def around(size, turn):
        return [(j, (j + turn) % size) for j in range(size)]

    col_pieces = [lax.ppermute(samples, grid_axes, from_row_line(turn)) for turn in span]
    beside = [lax.ppermute(samples, "col", around(cols, turn)) for turn in range(1, cols)]
    place, own, own_diag, held, high, low = prepare(place, samples, diag_tiles, tiles)
    kept, sent, panel = partial_image(
        place, tile_count, own, own_diag, high, low, col_pieces, beside
    )
    swapped = lax.ppermute(sent, "rep", around(2, 1))
    chip = kept + swapped[:cols]
    image = chip
    for turn in range(1, cols):
        image = image + lax.ppermute(chip, "col", around(cols, turn))

    def to_row(turn):
        return [
            (line * groups + j, (groups - 1 - j if turn else j) * groups + line)
            for line in span
            for j in span
        ]

    first, second = [lax.ppermute(image, grid_axes, to_row(turn)) for turn in range(2)]
    other = lax.ppermute(image, "rep", around(2, 1))
    left_high, left_low, new_diag = middle(
        image, other, own, own_diag, swapped, beside
    )
    new_slots = update_slots(
        place, tile_count, left_high, left_low, panel, first, second, held
    )
    return new_slots.reshape(omega_slots.shape), new_diag


def solution(mesh):
    placed = (
        P("parts", ("row", "col", "rep")),
        P(("parts", "row", "col", "rep"), None, None),
        P(("parts", "row"), ("col", "rep"), None, None, None),
        P(("parts", "row"), ("col", "rep"), None, None),
        P(("parts", "row"), ("col", "rep")),
    )
    return jax.shard_map(
        on_device,
        mesh=mesh,
        in_specs=placed,
        out_specs=(
            P(("parts", "row"), ("col", "rep"), None, None, None),
            P(("parts", "row", "col", "rep"), None, None),
        ),
        check_vma=False,
    )
```

```python
import functools

import jax
import jax.numpy as jnp
from jax import lax
from jax.experimental import pallas as pl
from jax.experimental.pallas import tpu as pltpu
from jax.sharding import PartitionSpec as P

step_size = 1.0
penalty = 0.1
grid_axes = ("row", "col", "rep")
line_axes = ("col", "rep")
f32 = jnp.float32
bf16 = jnp.bfloat16
vmem = pl.BlockSpec(memory_space=pltpu.VMEM)
smem = pl.BlockSpec(memory_space=pltpu.SMEM)
hbm = pl.BlockSpec(memory_space=pltpu.HBM)
room = pltpu.CompilerParams(vmem_limit_bytes=24 * 2**20)


def halves(values):
    high = values.astype(bf16)
    return high, (values - high.astype(f32)).astype(bf16)


def dot(left, right, dims):
    return lax.dot_general(left, right, (dims, ((), ())), preferred_element_type=f32)


def soft_limit(values):
    limit_value = step_size * penalty
    return values - jnp.clip(values, -limit_value, limit_value)


def prepare_kernel(*refs):
    slots = refs[3].shape[0]
    sources, targets = refs[:4], refs[4:8]
    high, low, sems = refs[8:]
    tiles, held = sources[3], targets[3]
    copies = [
        pltpu.make_async_copy(tiles.at[slot], held.at[slot], sems.at[slot])
        for slot in range(slots)
    ]
    for turn in range(3):
        copies.append(pltpu.make_async_copy(sources[turn], targets[turn], sems.at[slots + turn]))
    for copy in copies:
        copy.start()
    for slot in range(slots):
        copies[slot].wait()
        high[slot], low[slot] = halves(held[slot])
    for copy in copies[slots:]:
        copy.wait()


def prepare(*arrays):
    held = [jax.ShapeDtypeStruct(x.shape, x.dtype) for x in arrays]
    half = jax.ShapeDtypeStruct(arrays[-1].shape, bf16)
    return pl.pallas_call(
        prepare_kernel,
        out_shape=(*held, half, half),
        in_specs=[hbm] * 4,
        out_specs=(smem,) + (vmem,) * 5,
        scratch_shapes=[pltpu.SemaphoreType.DMA((arrays[-1].shape[0] + 3,))],
        compiler_params=room,
        name="prepare",
    )(*[pltpu.with_memory_space_constraint(x, pltpu.HBM) for x in arrays])


def partial_kernel(groups, place, count, samples, diag, high, low, *refs):
    pieces = refs[:groups]
    beside = refs[groups:-4]
    kept, sent, panel, total = refs[-4:]
    row = lax.axis_index("row")
    col = lax.axis_index("col")
    rep = lax.axis_index("rep")
    rows = samples.shape[0]
    for turn in range(groups):
        spot = lax.rem(row + turn, groups)
        block = 2 * lax.rem(spot, groups // 2) + lax.div(spot, groups // 2)
        panel[block, :rows], panel[block, rows:] = halves(pieces[turn][...])
    total[...] = jnp.zeros_like(total)

    def term(x_high, both, w_high, w_low, dims):
        wide = dot(both, w_high, dims)
        return wide[:rows] + wide[rows:] + dot(x_high, w_low, dims)

    own_high, own_low = halves(samples[...])
    total[col * 2 + rep] = term(
        own_high, jnp.concatenate([own_high, own_low], axis=0), *halves(diag[0]), ((1,), (0,))
    )
    for slot in range(high.shape[0]):
        source = panel.at[place[1, slot]]
        value = term(source[:rows], source[...], high[slot], low[slot], ((1,), (1,)))
        total[place[0, slot]] += jnp.where(slot < count[0, 0], value, 0.0)
    for pair in range(groups // 2):
        kept[pair] = total[2 * pair + rep]
        sent[pair] = total[2 * pair + 1 - rep]
    for turn, piece in enumerate((samples, *beside)):
        sent[groups // 2 + turn] = piece[...]


def partial_image(place, count, samples, diag, high, low, pieces, beside):
    groups = len(pieces)
    rows, side = samples.shape
    kept = jax.ShapeDtypeStruct((groups // 2, rows, side), f32)
    sent = jax.ShapeDtypeStruct((groups, rows, side), f32)
    panel = jax.ShapeDtypeStruct((groups, 2 * rows, side), bf16)
    return pl.pallas_call(
        functools.partial(partial_kernel, groups),
        out_shape=(kept, sent, panel),
        in_specs=[smem, smem] + [vmem] * (3 + groups + groups // 2),
        out_specs=(vmem, vmem, vmem),
        scratch_shapes=[pltpu.VMEM((groups, rows, side), f32)],
        compiler_params=room,
        name="partial_image",
    )(place, count, samples, diag, high, low, *pieces, *beside)


def middle_kernel(own_image, other_image, samples, diag, swapped, *refs):
    beside = refs[:-5]
    high, low, new_diag, shifted, sem = refs[-5:]
    pairs = own_image.shape[0]
    rep = lax.axis_index("rep")
    col = lax.axis_index("col")
    rows, side = samples.shape
    half = high.shape[2] // 2
    blank = jnp.zeros((side, half - rows), bf16)
    for turn, piece in enumerate((samples, *beside)):
        line = 2 * lax.rem(col + pairs - turn, pairs)
        for block, values in ((line + rep, piece[...]), (line + 1 - rep, swapped[pairs + turn])):
            for ref, part in zip((high, low), halves(values.T)):
                ref[block, :, :rows] = part
                ref[block, :, rows:half] = blank
                ref[block, :, half + rows :] = blank
    left_high, left_low = halves(samples[...].T)
    right_high, right_low = halves(own_image[col])
    dims = ((1,), (0,))
    one_side = dot(left_high, right_high, dims) + dot(left_low, right_high, dims)
    one_side += dot(left_high, right_low, dims)
    tile = diag[0]
    line = lax.broadcasted_iota(jnp.int32, (side, side), 0)
    on_diag = line == lax.broadcasted_iota(jnp.int32, (side, side), 1)
    gradient = (one_side + one_side.T) * (1.0 / (2.0 * rows))
    moved = tile - step_size * gradient
    inverse = step_size / jnp.where(on_diag, tile, 1.0)
    shifted[0] = jnp.where(on_diag, moved + inverse, soft_limit(moved))
    copy = pltpu.make_async_copy(shifted, new_diag, sem)
    copy.start()
    for pair in range(pairs):
        for parity, image in ((rep, own_image), (1 - rep, other_image)):
            block = 2 * pair + parity
            image_high, image_low = halves(image[pair].T)
            high[block, :, half : half + rows] = image_high
            low[block, :, half : half + rows] = image_low
    copy.wait()


def middle(own_image, other_image, samples, diag, swapped, beside):
    groups = swapped.shape[0]
    rows, side = samples.shape
    depth = 2 * -(-rows // 128) * 128
    left = jax.ShapeDtypeStruct((groups, side, depth), bf16)
    return pl.pallas_call(
        middle_kernel,
        out_shape=(left, left, jax.ShapeDtypeStruct(diag.shape, f32)),
        in_specs=[vmem] * (5 + len(beside)),
        out_specs=(vmem, vmem, hbm),
        scratch_shapes=[pltpu.VMEM(diag.shape, f32), pltpu.SemaphoreType.DMA],
        compiler_params=room,
        name="middle",
    )(own_image, other_image, samples, diag, swapped, *beside)


def slots_kernel(
    place, count, left_high, left_low, panel, first, second, tiles, out, high, low, ready, sems
):
    groups = panel.shape[0]
    rows = panel.shape[1] // 2
    half = high.shape[1] // 2
    parity = lax.div(lax.axis_index("row"), groups // 2)
    for ref in (high, low):
        for start in (rows, half + rows):
            blank = jnp.zeros((groups, half - rows, high.shape[2]), bf16)
            ref[:, start : start + half - rows] = blank
    for pair in range(groups // 2):
        for turn, piece in enumerate((first, second)):
            block = 2 * pair + (1 - parity if turn else parity)
            high[block, :rows], low[block, :rows] = halves(piece[pair])
    high[:, half : half + rows] = panel[:, :rows]
    low[:, half : half + rows] = panel[:, rows:]
    dims = ((1,), (0,))
    copies = []
    for slot in range(tiles.shape[0]):
        left, right = place[0, slot], place[1, slot]
        gradient = dot(left_high[left], high[right], dims)
        gradient += dot(left_low[left], high[right], dims)
        gradient += dot(left_high[left], low[right], dims)
        value = soft_limit(tiles[slot] - gradient * (step_size / (2.0 * rows)))
        ready[slot] = jnp.where(slot < count[0, 0], value, 0.0)
        copies.append(pltpu.make_async_copy(ready.at[slot], out.at[slot], sems.at[slot]))
        copies[-1].start()
    for copy in copies:
        copy.wait()


def update_slots(place, count, left_high, left_low, panel, first, second, tiles):
    slots, side, _ = tiles.shape
    groups, _, depth = left_high.shape
    return pl.pallas_call(
        slots_kernel,
        out_shape=jax.ShapeDtypeStruct(tiles.shape, f32),
        in_specs=[smem, smem] + [vmem] * 6,
        out_specs=hbm,
        scratch_shapes=[
            pltpu.VMEM((groups, depth, side), bf16),
            pltpu.VMEM((groups, depth, side), bf16),
            pltpu.VMEM(tiles.shape, f32),
            pltpu.SemaphoreType.DMA((slots,)),
        ],
        compiler_params=room,
        name="update_slots",
    )(place, count, left_high, left_low, panel, first, second, tiles)


def on_device(samples, diag_tiles, omega_slots, tile_pos, tile_count):
    groups = lax.axis_size(line_axes)
    cols = lax.axis_size("col")
    slots, side = omega_slots.shape[2], omega_slots.shape[3]
    tiles = omega_slots.reshape(slots, side, side)
    place = tile_pos.reshape(slots, 2).T
    span = range(groups)

    def from_row_line(turn):
        return [
            (line * groups + j, (j // 2 + cols * (j % 2) - turn) % groups * groups + line)
            for line in span
            for j in span
        ]

    def around(size, turn):
        return [(j, (j + turn) % size) for j in range(size)]

    col_pieces = [lax.ppermute(samples, grid_axes, from_row_line(turn)) for turn in span]
    beside = [lax.ppermute(samples, "col", around(cols, turn)) for turn in range(1, cols)]
    place, own, own_diag, held, high, low = prepare(place, samples, diag_tiles, tiles)
    kept, sent, panel = partial_image(
        place, tile_count, own, own_diag, high, low, col_pieces, beside
    )
    swapped = lax.ppermute(sent, "rep", around(2, 1))
    chip = kept + swapped[:cols]
    image = chip
    for turn in range(1, cols):
        image = image + lax.ppermute(chip, "col", around(cols, turn))

    def to_row(turn):
        return [
            (line * groups + j, (groups - 1 - spot if turn else spot) * groups + line)
            for line in span
            for j, spot in enumerate(x + cols * r for x in range(cols) for r in range(2))
        ]

    first, second = [lax.ppermute(image, grid_axes, to_row(turn)) for turn in range(2)]
    other = lax.ppermute(image, "rep", around(2, 1))
    left_high, left_low, new_diag = middle(
        image, other, own, own_diag, swapped, beside
    )
    new_slots = update_slots(
        place, tile_count, left_high, left_low, panel, first, second, held
    )
    return new_slots.reshape(omega_slots.shape), new_diag


def solution(mesh):
    placed = (
        P("parts", ("row", "col", "rep")),
        P(("parts", "row", "col", "rep"), None, None),
        P(("parts", "row"), ("col", "rep"), None, None, None),
        P(("parts", "row"), ("col", "rep"), None, None),
        P(("parts", "row"), ("col", "rep")),
    )
    return jax.shard_map(
        on_device,
        mesh=mesh,
        in_specs=placed,
        out_specs=(
            P(("parts", "row"), ("col", "rep"), None, None, None),
            P(("parts", "row", "col", "rep"), None, None),
        ),
        check_vma=False,
    )
```

```python
import functools

import jax
import jax.numpy as jnp
from jax import lax
from jax.experimental import pallas as pl
from jax.experimental.pallas import tpu as pltpu
from jax.sharding import PartitionSpec as P

step_size = 1.0
penalty = 0.1
grid_axes = ("row", "col", "rep")
line_axes = ("col", "rep")
f32 = jnp.float32
bf16 = jnp.bfloat16
vmem = pl.BlockSpec(memory_space=pltpu.VMEM)
smem = pl.BlockSpec(memory_space=pltpu.SMEM)
hbm = pl.BlockSpec(memory_space=pltpu.HBM)
room = pltpu.CompilerParams(vmem_limit_bytes=24 * 2**20)


def halves(values):
    high = values.astype(bf16)
    return high, (values - high.astype(f32)).astype(bf16)


def dot(left, right, dims):
    return lax.dot_general(left, right, (dims, ((), ())), preferred_element_type=f32)


def soft_limit(values):
    limit_value = step_size * penalty
    return values - jnp.clip(values, -limit_value, limit_value)


def sample_source(turn, row, own):
    return 2 * own - row - turn


def image_source(turn, row, own):
    return 2 * own - 1 - row if turn else row - 2 * own


def prepare_kernel(groups, place, count, *refs):
    arrays, (guide, *held), (high, low, sems) = refs[:3], refs[3:7], refs[7:]
    tiles = held[2]
    slots = tiles.shape[0]
    copies = [
        pltpu.make_async_copy(arrays[2].at[slot], tiles.at[slot], sems.at[slot])
        for slot in range(slots)
    ]
    for turn in range(2):
        copies.append(pltpu.make_async_copy(arrays[turn], held[turn], sems.at[slots + turn]))
    for copy in copies:
        copy.start()
    for slot in range(slots):
        guide[0, slot] = place[0, slot]
        guide[1, slot] = place[1, slot]
    row = lax.axis_index("row")
    own = lax.axis_index("col") * 2 + lax.axis_index("rep")
    for turn in range(groups):
        guide[2, turn] = lax.rem(sample_source(turn, row, own) + 4 * groups, groups)
    for turn in range(2):
        guide[3, turn] = lax.rem(image_source(turn, row, own) + 4 * groups, 2)
    guide[4, 0] = count[0, 0]
    for slot in range(slots):
        copies[slot].wait()
        high[slot], low[slot] = halves(tiles[slot])
    for copy in copies[slots:]:
        copy.wait()


def prepare(groups, place, count, *arrays):
    width = max(place.shape[1], groups)
    held = [jax.ShapeDtypeStruct(x.shape, x.dtype) for x in arrays]
    half = jax.ShapeDtypeStruct(arrays[-1].shape, bf16)
    return pl.pallas_call(
        functools.partial(prepare_kernel, groups),
        out_shape=(pltpu.SMEM((5, width), jnp.int32), *held, half, half),
        in_specs=[smem] * 2 + [hbm] * 3,
        out_specs=(smem,) + (vmem,) * 5,
        scratch_shapes=[pltpu.SemaphoreType.DMA((arrays[-1].shape[0] + 2,))],
        compiler_params=room,
        name="prepare",
    )(
        place,
        count,
        *[pltpu.with_memory_space_constraint(x, pltpu.HBM) for x in arrays],
    )


def partial_kernel(groups, guide, samples, diag, high, low, *refs):
    pieces = refs[:groups]
    beside = refs[groups:-4]
    kept, sent, panel, total = refs[-4:]
    col = lax.axis_index("col")
    rep = lax.axis_index("rep")
    rows = samples.shape[0]
    for turn in range(groups):
        block = guide[2, turn]
        panel[block, :rows], panel[block, rows:] = halves(pieces[turn][...])
    total[...] = jnp.zeros_like(total)

    def term(x_high, both, w_high, w_low, dims):
        wide = dot(both, w_high, dims)
        return wide[:rows] + wide[rows:] + dot(x_high, w_low, dims)

    own_high, own_low = halves(samples[...])
    total[col * 2 + rep] = term(
        own_high, jnp.concatenate([own_high, own_low], axis=0), *halves(diag[0]), ((1,), (0,))
    )
    for slot in range(high.shape[0]):
        source = panel.at[guide[1, slot]]
        value = term(source[:rows], source[...], high[slot], low[slot], ((1,), (1,)))
        total[guide[0, slot]] += jnp.where(slot < guide[4, 0], value, 0.0)
    for pair in range(groups // 2):
        kept[pair] = total[2 * pair + rep]
        sent[pair] = total[2 * pair + 1 - rep]
    for turn, piece in enumerate((samples, *beside)):
        sent[groups // 2 + turn] = piece[...]


def partial_image(guide, samples, diag, high, low, pieces, beside):
    groups = len(pieces)
    rows, side = samples.shape
    kept = jax.ShapeDtypeStruct((groups // 2, rows, side), f32)
    sent = jax.ShapeDtypeStruct((groups, rows, side), f32)
    panel = jax.ShapeDtypeStruct((groups, 2 * rows, side), bf16)
    return pl.pallas_call(
        functools.partial(partial_kernel, groups),
        out_shape=(kept, sent, panel),
        in_specs=[smem] + [vmem] * (3 + groups + groups // 2),
        out_specs=(vmem, vmem, vmem),
        scratch_shapes=[pltpu.VMEM((groups, rows, side), f32)],
        compiler_params=room,
        name="partial_image",
    )(guide, samples, diag, high, low, *pieces, *beside)


def middle_kernel(own_image, other_image, samples, diag, swapped, *refs):
    beside = refs[:-5]
    high, low, new_diag, shifted, sem = refs[-5:]
    pairs = own_image.shape[0]
    rep = lax.axis_index("rep")
    col = lax.axis_index("col")
    rows, side = samples.shape
    half = high.shape[2] // 2
    blank = jnp.zeros((side, half - rows), bf16)
    for turn, piece in enumerate((samples, *beside)):
        line = 2 * lax.rem(col + pairs - turn, pairs)
        for block, values in ((line + rep, piece[...]), (line + 1 - rep, swapped[pairs + turn])):
            for ref, part in zip((high, low), halves(values.T)):
                ref[block, :, :rows] = part
                ref[block, :, rows:half] = blank
                ref[block, :, half + rows :] = blank
    left_high, left_low = halves(samples[...].T)
    right_high, right_low = halves(own_image[col])
    dims = ((1,), (0,))
    one_side = dot(left_high, right_high, dims) + dot(left_low, right_high, dims)
    one_side += dot(left_high, right_low, dims)
    tile = diag[0]
    line = lax.broadcasted_iota(jnp.int32, (side, side), 0)
    on_diag = line == lax.broadcasted_iota(jnp.int32, (side, side), 1)
    gradient = (one_side + one_side.T) * (1.0 / (2.0 * rows))
    moved = tile - step_size * gradient
    inverse = step_size / jnp.where(on_diag, tile, 1.0)
    shifted[0] = jnp.where(on_diag, moved + inverse, soft_limit(moved))
    copy = pltpu.make_async_copy(shifted, new_diag, sem)
    copy.start()
    for pair in range(pairs):
        for parity, image in ((rep, own_image), (1 - rep, other_image)):
            block = 2 * pair + parity
            image_high, image_low = halves(image[pair].T)
            high[block, :, half : half + rows] = image_high
            low[block, :, half : half + rows] = image_low
    copy.wait()


def middle(own_image, other_image, samples, diag, swapped, beside):
    groups = swapped.shape[0]
    rows, side = samples.shape
    depth = 2 * -(-rows // 128) * 128
    left = jax.ShapeDtypeStruct((groups, side, depth), bf16)
    return pl.pallas_call(
        middle_kernel,
        out_shape=(left, left, jax.ShapeDtypeStruct(diag.shape, f32)),
        in_specs=[vmem] * (5 + len(beside)),
        out_specs=(vmem, vmem, hbm),
        scratch_shapes=[pltpu.VMEM(diag.shape, f32), pltpu.SemaphoreType.DMA],
        compiler_params=room,
        name="middle",
    )(own_image, other_image, samples, diag, swapped, *beside)


def slots_kernel(
    guide, left_high, left_low, panel, first, second, tiles, out, high, low, ready, sems
):
    groups = panel.shape[0]
    rows = panel.shape[1] // 2
    half = high.shape[1] // 2
    for ref in (high, low):
        for start in (rows, half + rows):
            blank = jnp.zeros((groups, half - rows, high.shape[2]), bf16)
            ref[:, start : start + half - rows] = blank
    for pair in range(groups // 2):
        for turn, piece in enumerate((first, second)):
            block = 2 * pair + guide[3, turn]
            high[block, :rows], low[block, :rows] = halves(piece[pair])
    high[:, half : half + rows] = panel[:, :rows]
    low[:, half : half + rows] = panel[:, rows:]
    dims = ((1,), (0,))
    copies = []
    for slot in range(tiles.shape[0]):
        left, right = guide[0, slot], guide[1, slot]
        gradient = dot(left_high[left], high[right], dims)
        gradient += dot(left_low[left], high[right], dims)
        gradient += dot(left_high[left], low[right], dims)
        value = soft_limit(tiles[slot] - gradient * (step_size / (2.0 * rows)))
        ready[slot] = jnp.where(slot < guide[4, 0], value, 0.0)
        copies.append(pltpu.make_async_copy(ready.at[slot], out.at[slot], sems.at[slot]))
        copies[-1].start()
    for copy in copies:
        copy.wait()


def update_slots(guide, left_high, left_low, panel, first, second, tiles):
    slots, side, _ = tiles.shape
    groups, _, depth = left_high.shape
    return pl.pallas_call(
        slots_kernel,
        out_shape=jax.ShapeDtypeStruct(tiles.shape, f32),
        in_specs=[smem] + [vmem] * 6,
        out_specs=hbm,
        scratch_shapes=[
            pltpu.VMEM((groups, depth, side), bf16),
            pltpu.VMEM((groups, depth, side), bf16),
            pltpu.VMEM(tiles.shape, f32),
            pltpu.SemaphoreType.DMA((slots,)),
        ],
        compiler_params=room,
        name="update_slots",
    )(guide, left_high, left_low, panel, first, second, tiles)


def on_device(samples, diag_tiles, omega_slots, tile_pos, tile_count):
    groups = lax.axis_size(line_axes)
    cols = lax.axis_size("col")
    slots, side = omega_slots.shape[2], omega_slots.shape[3]
    tiles = omega_slots.reshape(slots, side, side)
    place = tile_pos.reshape(slots, 2).T
    span = range(groups)

    def links(source, turn):
        return [
            (line * groups + source(turn, row, line) % groups, row * groups + line)
            for line in span
            for row in span
        ]

    def around(size, turn):
        return [(j, (j + turn) % size) for j in range(size)]

    col_pieces = [
        lax.ppermute(samples, grid_axes, links(sample_source, turn)) for turn in span
    ]
    beside = [lax.ppermute(samples, "col", around(cols, turn)) for turn in range(1, cols)]
    guide, own, own_diag, held, high, low = prepare(
        groups, place, tile_count, samples, diag_tiles, tiles
    )
    kept, sent, panel = partial_image(guide, own, own_diag, high, low, col_pieces, beside)
    swapped = lax.ppermute(sent, "rep", around(2, 1))
    chip = kept + swapped[:cols]
    image = chip
    for turn in range(1, cols):
        image = image + lax.ppermute(chip, "col", around(cols, turn))

    first, second = [
        lax.ppermute(image, grid_axes, links(image_source, turn)) for turn in range(2)
    ]
    other = lax.ppermute(image, "rep", around(2, 1))
    left_high, left_low, new_diag = middle(image, other, own, own_diag, swapped, beside)
    new_slots = update_slots(guide, left_high, left_low, panel, first, second, held)
    return new_slots.reshape(omega_slots.shape), new_diag


def solution(mesh):
    placed = (
        P("parts", ("row", "col", "rep")),
        P(("parts", "row", "col", "rep"), None, None),
        P(("parts", "row"), ("col", "rep"), None, None, None),
        P(("parts", "row"), ("col", "rep"), None, None),
        P(("parts", "row"), ("col", "rep")),
    )
    return jax.shard_map(
        on_device,
        mesh=mesh,
        in_specs=placed,
        out_specs=(
            P(("parts", "row"), ("col", "rep"), None, None, None),
            P(("parts", "row", "col", "rep"), None, None),
        ),
        check_vma=False,
    )
```

```python
import functools

import jax
import jax.numpy as jnp
from jax import lax
from jax.experimental import pallas as pl
from jax.experimental.pallas import tpu as pltpu
from jax.sharding import PartitionSpec as P

step_size = 1.0
penalty = 0.1
grid_axes = ("row", "col", "rep")
line_axes = ("col", "rep")
f32 = jnp.float32
bf16 = jnp.bfloat16
vmem = pl.BlockSpec(memory_space=pltpu.VMEM)
smem = pl.BlockSpec(memory_space=pltpu.SMEM)
hbm = pl.BlockSpec(memory_space=pltpu.HBM)
room = pltpu.CompilerParams(vmem_limit_bytes=24 * 2**20)


def halves(values):
    high = values.astype(bf16)
    return high, (values - high.astype(f32)).astype(bf16)


def dot(left, right, dims):
    return lax.dot_general(left, right, (dims, ((), ())), preferred_element_type=f32)


def soft_limit(values):
    limit_value = step_size * penalty
    return values - jnp.clip(values, -limit_value, limit_value)


def first_source(row, own, groups):
    rep = (row // 2 ^ row ^ own // (groups // 2)) & 1
    return 2 * (row // 2 ^ rep) + rep


def sample_source(turn, row, own, groups):
    return first_source(row, own, groups) ^ (2 * turn + turn % 2)


def image_source(turn, row, own, groups):
    return first_source(row, own, groups) ^ (turn * (groups - 1))


def prepare_kernel(groups, *refs):
    place, count, *arrays = refs[:4]
    guide, *held, high, low, spots, live, sems = refs[4:]
    tiles = held[1]
    slots = tiles.shape[0]
    pairs = [(place, spots), (count, live), (arrays[0], held[0])]
    pairs += [(arrays[1].at[slot], tiles.at[slot]) for slot in range(slots)]
    copies = [pltpu.make_async_copy(*pair, sems.at[i]) for i, pair in enumerate(pairs)]
    for copy in copies:
        copy.start()
    row = lax.axis_index("row")
    own = lax.axis_index("col") * 2 + lax.axis_index("rep")
    for turn in range(groups // 2):
        guide[2, turn] = sample_source(turn, row, own, groups)
    for turn in range(2):
        guide[3, turn] = image_source(turn, row, own, groups) & 1
    for slot in range(slots):
        copies[3 + slot].wait()
        high[slot], low[slot] = halves(tiles[slot])
    for copy in copies[:3]:
        copy.wait()
    for slot in range(slots):
        guide[0, slot] = spots[0, slot]
        guide[1, slot] = spots[1, slot]
    guide[4, 0] = live[0, 0]


def prepare(groups, *arrays):
    slots = arrays[-1].shape[0]
    width = max(slots, groups)
    held = [jax.ShapeDtypeStruct(x.shape, x.dtype) for x in arrays[2:]]
    half = jax.ShapeDtypeStruct(arrays[-1].shape, bf16)
    return pl.pallas_call(
        functools.partial(prepare_kernel, groups),
        out_shape=(pltpu.SMEM((5, width), jnp.int32), *held, half, half),
        in_specs=[hbm, vmem, hbm, hbm],
        out_specs=(smem,) + (vmem,) * 4,
        scratch_shapes=[
            pltpu.SMEM(arrays[0].shape, jnp.int32),
            pltpu.SMEM(arrays[1].shape, jnp.int32),
            pltpu.SemaphoreType.DMA((slots + 3,)),
        ],
        compiler_params=room,
        name="prepare",
    )(*[x if i == 1 else pltpu.with_memory_space_constraint(x, pltpu.HBM) for i, x in enumerate(arrays)])


def partial_kernel(guide, samples, diag, high, low, *refs):
    pieces = refs[:-4]
    groups = 2 * len(pieces)
    kept, sent, panel, total = refs[-4:]
    col = lax.axis_index("col")
    rep = lax.axis_index("rep")
    rows = samples.shape[1]
    for turn, piece in enumerate(pieces):
        for half in range(2):
            block = guide[2, turn] ^ half
            panel[block, :rows], panel[block, rows:] = halves(piece[half])
    total[...] = jnp.zeros_like(total)

    def term(x_high, both, w_high, w_low, dims):
        wide = dot(both, w_high, dims)
        return wide[:rows] + wide[rows:] + dot(x_high, w_low, dims)

    own_high, own_low = halves(samples[0])
    total[col * 2 + rep] = term(
        own_high, jnp.concatenate([own_high, own_low], axis=0), *halves(diag[0]), ((1,), (0,))
    )
    for slot in range(high.shape[0]):
        source = panel.at[guide[1, slot]]
        value = term(source[:rows], source[...], high[slot], low[slot], ((1,), (1,)))
        total[guide[0, slot]] += jnp.where(slot < guide[4, 0], value, 0.0)
    for pair in range(groups // 2):
        kept[pair] = total[2 * pair + rep]
        sent[pair] = total[2 * pair + 1 - rep]


def partial_image(guide, samples, diag, high, low, pieces):
    groups = 2 * len(pieces)
    _, rows, side = samples.shape
    half = jax.ShapeDtypeStruct((groups // 2, rows, side), f32)
    panel = jax.ShapeDtypeStruct((groups, 2 * rows, side), bf16)
    return pl.pallas_call(
        partial_kernel,
        out_shape=(half, half, panel),
        in_specs=[smem] + [vmem] * (4 + len(pieces)),
        out_specs=(vmem, vmem, vmem),
        scratch_shapes=[pltpu.VMEM((groups, rows, side), f32)],
        compiler_params=room,
        name="partial_image",
    )(guide, samples, diag, high, low, *pieces)


def middle_kernel(own_image, other_image, diag, *refs):
    samples = refs[:-5]
    high, low, new_diag, shifted, sem = refs[-5:]
    pairs = own_image.shape[0]
    rep = lax.axis_index("rep")
    col = lax.axis_index("col")
    _, rows, side = samples[0].shape
    half = high.shape[2] // 2
    blank = jnp.zeros((side, half - rows), bf16)
    for turn, piece in enumerate(samples):
        line = 2 * lax.rem(col + pairs - turn, pairs)
        for block, place in ((line + rep, 0), (line + 1 - rep, 1)):
            for ref, part in zip((high, low), halves(piece[place].T)):
                ref[block, :, :rows] = part
                ref[block, :, rows:half] = blank
                ref[block, :, half + rows :] = blank
    left_high, left_low = halves(samples[0][0].T)
    right_high, right_low = halves(own_image[col])
    dims = ((1,), (0,))
    one_side = dot(left_high, right_high, dims) + dot(left_low, right_high, dims)
    one_side += dot(left_high, right_low, dims)
    tile = diag[0]
    line = lax.broadcasted_iota(jnp.int32, (side, side), 0)
    on_diag = line == lax.broadcasted_iota(jnp.int32, (side, side), 1)
    gradient = (one_side + one_side.T) * (1.0 / (2.0 * rows))
    moved = tile - step_size * gradient
    inverse = step_size / jnp.where(on_diag, tile, 1.0)
    shifted[0] = jnp.where(on_diag, moved + inverse, soft_limit(moved))
    copy = pltpu.make_async_copy(shifted, new_diag, sem)
    copy.start()
    for pair in range(pairs):
        for parity, image in ((rep, own_image), (1 - rep, other_image)):
            block = 2 * pair + parity
            image_high, image_low = halves(image[pair].T)
            high[block, :, half : half + rows] = image_high
            low[block, :, half : half + rows] = image_low
    copy.wait()


def middle(own_image, other_image, diag, samples):
    pairs, rows, side = own_image.shape
    groups = 2 * pairs
    depth = 2 * -(-rows // 128) * 128
    left = jax.ShapeDtypeStruct((groups, side, depth), bf16)
    return pl.pallas_call(
        middle_kernel,
        out_shape=(left, left, jax.ShapeDtypeStruct(diag.shape, f32)),
        in_specs=[vmem] * (3 + len(samples)),
        out_specs=(vmem, vmem, hbm),
        scratch_shapes=[pltpu.VMEM(diag.shape, f32), pltpu.SemaphoreType.DMA],
        compiler_params=room,
        name="middle",
    )(own_image, other_image, diag, *samples)


def slots_kernel(
    guide, left_high, left_low, panel, first, second, tiles, out, high, low, ready, sems
):
    groups = panel.shape[0]
    rows = panel.shape[1] // 2
    half = high.shape[1] // 2
    for ref in (high, low):
        for start in (rows, half + rows):
            blank = jnp.zeros((groups, half - rows, high.shape[2]), bf16)
            ref[:, start : start + half - rows] = blank
    for pair in range(groups // 2):
        for turn, piece in enumerate((first, second)):
            block = 2 * pair + guide[3, turn]
            high[block, :rows], low[block, :rows] = halves(piece[pair])
    high[:, half : half + rows] = panel[:, :rows]
    low[:, half : half + rows] = panel[:, rows:]
    dims = ((1,), (0,))
    copies = []
    for slot in range(tiles.shape[0]):
        left, right = guide[0, slot], guide[1, slot]
        gradient = dot(left_high[left], high[right], dims)
        gradient += dot(left_low[left], high[right], dims)
        gradient += dot(left_high[left], low[right], dims)
        value = soft_limit(tiles[slot] - gradient * (step_size / (2.0 * rows)))
        ready[slot] = jnp.where(slot < guide[4, 0], value, 0.0)
        copies.append(pltpu.make_async_copy(ready.at[slot], out.at[slot], sems.at[slot]))
        copies[-1].start()
    for copy in copies:
        copy.wait()


def update_slots(guide, left_high, left_low, panel, first, second, tiles):
    slots, side, _ = tiles.shape
    groups, _, depth = left_high.shape
    return pl.pallas_call(
        slots_kernel,
        out_shape=jax.ShapeDtypeStruct(tiles.shape, f32),
        in_specs=[smem] + [vmem] * 6,
        out_specs=hbm,
        scratch_shapes=[
            pltpu.VMEM((groups, depth, side), bf16),
            pltpu.VMEM((groups, depth, side), bf16),
            pltpu.VMEM(tiles.shape, f32),
            pltpu.SemaphoreType.DMA((slots,)),
        ],
        compiler_params=room,
        name="update_slots",
    )(guide, left_high, left_low, panel, first, second, tiles)


def on_device(samples, diag_tiles, omega_slots, tile_pos, tile_count):
    groups = lax.axis_size(line_axes)
    cols = lax.axis_size("col")
    slots, side = omega_slots.shape[2], omega_slots.shape[3]
    tiles = omega_slots.reshape(slots, side, side)
    place = tile_pos.reshape(slots, 2).T
    span = range(groups)

    def links(source, turn):
        return [
            (line * groups + source(turn, row, line, groups), row * groups + line)
            for line in span
            for row in span
        ]

    def around(size, turn):
        return [(j, (j + turn) % size) for j in range(size)]

    pair = jnp.stack([samples, lax.ppermute(samples, "rep", around(2, 1))])
    col_pieces = [
        lax.ppermute(pair, grid_axes, links(sample_source, turn)) for turn in range(cols)
    ]
    guide, own_diag, held, high, low = prepare(groups, place, tile_count, diag_tiles, tiles)
    kept, sent, panel = partial_image(guide, pair, own_diag, high, low, col_pieces)
    chip = kept + lax.ppermute(sent, "rep", around(2, 1))
    image = chip
    for turn in range(1, cols):
        image = image + lax.ppermute(chip, "col", around(cols, turn))

    late, image = lax.optimization_barrier((pair, image))
    beside = [lax.ppermute(late, "col", around(cols, turn)) for turn in range(1, cols)]
    first, second = [
        lax.ppermute(image, grid_axes, links(image_source, turn)) for turn in range(2)
    ]
    other = lax.ppermute(image, "rep", around(2, 1))
    left_high, left_low, new_diag = middle(image, other, own_diag, [pair, *beside])
    new_slots = update_slots(guide, left_high, left_low, panel, first, second, held)
    return new_slots.reshape(omega_slots.shape), new_diag


def solution(mesh):
    placed = (
        P("parts", ("row", "col", "rep")),
        P(("parts", "row", "col", "rep"), None, None),
        P(("parts", "row"), ("col", "rep"), None, None, None),
        P(("parts", "row"), ("col", "rep"), None, None),
        P(("parts", "row"), ("col", "rep")),
    )
    return jax.shard_map(
        on_device,
        mesh=mesh,
        in_specs=placed,
        out_specs=(
            P(("parts", "row"), ("col", "rep"), None, None, None),
            P(("parts", "row", "col", "rep"), None, None),
        ),
        check_vma=False,
    )
```

```python
import functools

import jax
import jax.numpy as jnp
from jax import lax
from jax.experimental import pallas as pl
from jax.experimental.pallas import tpu as pltpu
from jax.sharding import PartitionSpec as P

step_size = 1.0
penalty = 0.1
grid_axes = ("row", "col", "rep")
line_axes = ("col", "rep")
f32 = jnp.float32
bf16 = jnp.bfloat16
vmem = pl.BlockSpec(memory_space=pltpu.VMEM)
smem = pl.BlockSpec(memory_space=pltpu.SMEM)
hbm = pl.BlockSpec(memory_space=pltpu.HBM)
room = pltpu.CompilerParams(vmem_limit_bytes=24 * 2**20)


def halves(values):
    high = values.astype(bf16)
    return high, (values - high.astype(f32)).astype(bf16)


def dot(left, right):
    return jnp.dot(left, right, preferred_element_type=f32)


def soft_limit(values):
    limit_value = step_size * penalty
    return values - jnp.clip(values, -limit_value, limit_value)


def first_source(row, own, groups):
    rep = (row // 2 ^ row ^ own // (groups // 2)) & 1
    return 2 * (row // 2 ^ rep) + rep


def sample_source(turn, row, own, groups):
    spot = groups // 2 - 1 - turn
    return first_source(row, own, groups) ^ (2 * spot + spot % 2)


def image_source(turn, row, own, groups):
    return first_source(row, own, groups) ^ ((1 - turn) * (groups - 1))


def prepare_kernel(groups, *refs):
    place, count, *arrays = refs[:4]
    guide, *held, high, low, spots, live, sems = refs[4:]
    tiles = held[1]
    slots = tiles.shape[0]
    pairs = [(place, spots), (count, live), (arrays[0], held[0])]
    pairs += [(arrays[1].at[slot], tiles.at[slot]) for slot in range(slots)]
    copies = [pltpu.make_async_copy(*pair, sems.at[i]) for i, pair in enumerate(pairs)]
    for copy in copies:
        copy.start()
    row = lax.axis_index("row")
    own = lax.axis_index("col") * 2 + lax.axis_index("rep")
    for turn in range(groups // 2):
        guide[2, turn] = sample_source(turn, row, own, groups)
    for turn in range(2):
        guide[3, turn] = image_source(turn, row, own, groups) & 1
    for slot in range(slots):
        copies[3 + slot].wait()
        high[slot], low[slot] = halves(tiles[slot].T)
    for copy in copies[:3]:
        copy.wait()
    for slot in range(slots):
        guide[0, slot] = spots[0, slot]
        guide[1, slot] = spots[1, slot]
    guide[4, 0] = live[0, 0]


def prepare(groups, *arrays):
    slots = arrays[-1].shape[0]
    width = max(slots, groups)
    held = [jax.ShapeDtypeStruct(x.shape, x.dtype) for x in arrays[2:]]
    half = jax.ShapeDtypeStruct(arrays[-1].shape, bf16)
    return pl.pallas_call(
        functools.partial(prepare_kernel, groups),
        out_shape=(pltpu.SMEM((5, width), jnp.int32), *held, half, half),
        in_specs=[hbm, vmem, hbm, hbm],
        out_specs=(smem,) + (vmem,) * 4,
        scratch_shapes=[
            pltpu.SMEM(arrays[0].shape, jnp.int32),
            pltpu.SMEM(arrays[1].shape, jnp.int32),
            pltpu.SemaphoreType.DMA((slots + 3,)),
        ],
        compiler_params=room,
        name="prepare",
    )(*[x if i == 1 else pltpu.with_memory_space_constraint(x, pltpu.HBM) for i, x in enumerate(arrays)])


def partial_kernel(guide, samples, diag, high, low, *refs):
    pieces = refs[:-4]
    groups = 2 * len(pieces)
    kept, sent, panel, total = refs[-4:]
    col = lax.axis_index("col")
    rep = lax.axis_index("rep")
    rows = samples.shape[1]
    for turn, piece in enumerate(pieces):
        for half in range(2):
            block = guide[2, turn] ^ half
            panel[block, :rows], panel[block, rows:] = halves(piece[half])
    total[...] = jnp.zeros_like(total)

    def term(x_high, both, w_high, w_low):
        wide = dot(both, w_high)
        return wide[:rows] + wide[rows:] + dot(x_high, w_low)

    own_high, own_low = halves(samples[0])
    total[col * 2 + rep] = term(
        own_high, jnp.concatenate([own_high, own_low], axis=0), *halves(diag[0])
    )
    for slot in range(high.shape[0]):
        source = panel.at[guide[1, slot]]
        value = term(source[:rows], source[...], high[slot], low[slot])
        total[guide[0, slot]] += jnp.where(slot < guide[4, 0], value, 0.0)
    for pair in range(groups // 2):
        kept[pair] = total[2 * pair + rep]
        sent[pair] = total[2 * pair + 1 - rep]


def partial_image(guide, samples, diag, high, low, pieces):
    groups = 2 * len(pieces)
    _, rows, side = samples.shape
    half = jax.ShapeDtypeStruct((groups // 2, rows, side), f32)
    panel = jax.ShapeDtypeStruct((groups, 2 * rows, side), bf16)
    return pl.pallas_call(
        partial_kernel,
        out_shape=(half, half, panel),
        in_specs=[smem] + [vmem] * (4 + len(pieces)),
        out_specs=(vmem, vmem, vmem),
        scratch_shapes=[pltpu.VMEM((groups, rows, side), f32)],
        compiler_params=room,
        name="partial_image",
    )(guide, samples, diag, high, low, *pieces)


def half_gradient_kernel(
    guide, own_image, other_image, samples, panel, diag, tiles, moved, new_diag, wide, low, step, sem
):
    pairs, rows, side = own_image.shape
    rep = lax.axis_index("rep")
    left_high, left_low = halves(samples[0].T)
    right_high, right_low = halves(own_image[lax.axis_index("col")])
    one_side = dot(left_high, right_high) + dot(left_low, right_high) + dot(left_high, right_low)
    tile = diag[0]
    line = lax.broadcasted_iota(jnp.int32, (side, side), 0)
    on_diag = line == lax.broadcasted_iota(jnp.int32, (side, side), 1)
    scale = step_size / (2.0 * rows)
    shifted = tile - (one_side + one_side.T) * scale
    inverse = step_size / jnp.where(on_diag, tile, 1.0)
    step[0] = jnp.where(on_diag, shifted + inverse, soft_limit(shifted))
    copy = pltpu.make_async_copy(step, new_diag, sem)
    copy.start()
    for pair in range(pairs):
        for parity, image in ((rep, own_image), (1 - rep, other_image)):
            block = 2 * pair + parity
            image_high, low[block] = halves(image[pair].T)
            wide[block, :, :rows] = image_high
            wide[block, :, rows:] = image_high
    for slot in range(tiles.shape[0]):
        left, right = guide[0, slot], guide[1, slot]
        gradient = dot(wide[left], panel[right]) + dot(low[left], panel[right, :rows])
        moved[slot] = tiles[slot] - gradient * scale
    copy.wait()


def half_gradient(guide, own_image, other_image, samples, panel, diag, tiles):
    groups, _, side = panel.shape
    rows = samples.shape[1]
    return pl.pallas_call(
        half_gradient_kernel,
        out_shape=(
            jax.ShapeDtypeStruct(tiles.shape, f32),
            jax.ShapeDtypeStruct(diag.shape, f32),
        ),
        in_specs=[smem] + [vmem] * 6,
        out_specs=(vmem, hbm),
        scratch_shapes=[
            pltpu.VMEM((groups, side, 2 * rows), bf16),
            pltpu.VMEM((groups, side, rows), bf16),
            pltpu.VMEM(diag.shape, f32),
            pltpu.SemaphoreType.DMA,
        ],
        compiler_params=room,
        name="half_gradient",
    )(guide, own_image, other_image, samples, panel, diag, tiles)


def row_panel_kernel(*refs):
    samples, (wide, low) = refs[:-2], refs[-2:]
    rep = lax.axis_index("rep")
    col = lax.axis_index("col")
    rows = samples[0].shape[1]
    pairs = len(samples)
    for turn, piece in enumerate(samples):
        line = 2 * lax.rem(col + pairs - turn, pairs)
        for block, place in ((line + rep, 0), (line + 1 - rep, 1)):
            high, low[block] = halves(piece[place].T)
            wide[block, :, :rows] = high
            wide[block, :, rows:] = high


def row_panel(samples):
    _, rows, side = samples[0].shape
    groups = 2 * len(samples)
    return pl.pallas_call(
        row_panel_kernel,
        out_shape=(
            jax.ShapeDtypeStruct((groups, side, 2 * rows), bf16),
            jax.ShapeDtypeStruct((groups, side, rows), bf16),
        ),
        in_specs=[vmem] * len(samples),
        out_specs=(vmem, vmem),
        compiler_params=room,
        name="row_panel",
    )(*samples)


def slots_kernel(guide, wide, low, first, second, moved, out, panel, ready, sems):
    pairs, rows, _ = first.shape
    for pair in range(pairs):
        for turn, piece in enumerate((first, second)):
            block = 2 * pair + guide[3, turn]
            panel[block, :rows], panel[block, rows:] = halves(piece[pair])
    copies = []
    for slot in range(moved.shape[0]):
        left, right = guide[0, slot], guide[1, slot]
        gradient = dot(wide[left], panel[right]) + dot(low[left], panel[right, :rows])
        value = soft_limit(moved[slot] - gradient * (step_size / (2.0 * rows)))
        ready[slot] = jnp.where(slot < guide[4, 0], value, 0.0)
        copies.append(pltpu.make_async_copy(ready.at[slot], out.at[slot], sems.at[slot]))
        copies[-1].start()
    for copy in copies:
        copy.wait()


def update_slots(guide, wide, low, first, second, moved):
    slots, side, _ = moved.shape
    groups, _, depth = wide.shape
    return pl.pallas_call(
        slots_kernel,
        out_shape=jax.ShapeDtypeStruct(moved.shape, f32),
        in_specs=[smem] + [vmem] * 5,
        out_specs=hbm,
        scratch_shapes=[
            pltpu.VMEM((groups, depth, side), bf16),
            pltpu.VMEM(moved.shape, f32),
            pltpu.SemaphoreType.DMA((slots,)),
        ],
        compiler_params=room,
        name="update_slots",
    )(guide, wide, low, first, second, moved)


def on_device(samples, diag_tiles, omega_slots, tile_pos, tile_count):
    groups = lax.axis_size(line_axes)
    cols = lax.axis_size("col")
    slots, side = omega_slots.shape[2], omega_slots.shape[3]
    tiles = omega_slots.reshape(slots, side, side)
    place = tile_pos.reshape(slots, 2).T
    span = range(groups)

    def links(source, turn):
        return [
            (line * groups + source(turn, row, line, groups), row * groups + line)
            for line in span
            for row in span
        ]

    def around(size, turn):
        return [(j, (j + turn) % size) for j in range(size)]

    pair = jnp.stack([samples, lax.ppermute(samples, "rep", around(2, 1))])
    col_pieces = [
        lax.ppermute(pair, grid_axes, links(sample_source, turn)) for turn in range(cols)
    ]
    guide, own_diag, held, high, low = prepare(groups, place, tile_count, diag_tiles, tiles)
    kept, sent, panel = partial_image(guide, pair, own_diag, high, low, col_pieces)
    chip = kept + lax.ppermute(sent, "rep", around(2, 1))
    image = chip
    for turn in range(1, cols):
        image = image + lax.ppermute(chip, "col", around(cols, turn))

    late, image = lax.optimization_barrier((pair, image))
    beside = [lax.ppermute(late, "col", around(cols, turn)) for turn in range(1, cols)]
    first, second = [
        lax.ppermute(image, grid_axes, links(image_source, turn)) for turn in range(2)
    ]
    other = lax.ppermute(image, "rep", around(2, 1))
    moved, new_diag = half_gradient(guide, image, other, pair, panel, own_diag, held)
    wide, low = row_panel([pair, *beside])
    new_slots = update_slots(guide, wide, low, first, second, moved)
    return new_slots.reshape(omega_slots.shape), new_diag


def solution(mesh):
    placed = (
        P("parts", ("row", "col", "rep")),
        P(("parts", "row", "col", "rep"), None, None),
        P(("parts", "row"), ("col", "rep"), None, None, None),
        P(("parts", "row"), ("col", "rep"), None, None),
        P(("parts", "row"), ("col", "rep")),
    )
    return jax.shard_map(
        on_device,
        mesh=mesh,
        in_specs=placed,
        out_specs=(
            P(("parts", "row"), ("col", "rep"), None, None, None),
            P(("parts", "row", "col", "rep"), None, None),
        ),
        check_vma=False,
    )
```

```python
import functools

import jax
import jax.numpy as jnp
from jax import lax
from jax.experimental import pallas as pl
from jax.experimental.pallas import tpu as pltpu
from jax.sharding import PartitionSpec as P

step_size = 1.0
penalty = 0.1
grid_axes = ("row", "col", "rep")
line_axes = ("col", "rep")
f32 = jnp.float32
bf16 = jnp.bfloat16
vmem = pl.BlockSpec(memory_space=pltpu.VMEM)
smem = pl.BlockSpec(memory_space=pltpu.SMEM)
hbm = pl.BlockSpec(memory_space=pltpu.HBM)
room = pltpu.CompilerParams(vmem_limit_bytes=24 * 2**20)


def halves(values):
    high = values.astype(bf16)
    return high, (values - high.astype(f32)).astype(bf16)


def dot(left, right):
    return jnp.dot(left, right, preferred_element_type=f32)


def soft_limit(values):
    limit_value = step_size * penalty
    return values - jnp.clip(values, -limit_value, limit_value)


def first_source(row, own, groups):
    rep = (row // 2 ^ row ^ own // (groups // 2)) & 1
    return 2 * (row // 2 ^ rep) + rep


def sample_source(turn, row, own, groups):
    spot = groups // 2 - 1 - turn
    return first_source(row, own, groups) ^ (2 * spot + spot % 2)


def image_source(turn, row, own, groups):
    return first_source(row, own, groups) ^ ((1 - turn) * (groups - 1))


def prepare_kernel(groups, *refs):
    place, count, *arrays = refs[:4]
    guide, *held, high, low, spots, live, sems = refs[4:]
    tiles = held[1]
    slots = tiles.shape[0]
    pairs = [(place, spots), (count, live), (arrays[0], held[0])]
    pairs += [(arrays[1].at[slot], tiles.at[slot]) for slot in range(slots)]
    copies = [pltpu.make_async_copy(*pair, sems.at[i]) for i, pair in enumerate(pairs)]
    for copy in copies:
        copy.start()
    row = lax.axis_index("row")
    own = lax.axis_index("col") * 2 + lax.axis_index("rep")
    for turn in range(groups // 2):
        guide[2, turn] = sample_source(turn, row, own, groups)
    for turn in range(2):
        guide[3, turn] = image_source(turn, row, own, groups) & 1
    for slot in range(slots):
        copies[3 + slot].wait()
        high[slot], low[slot] = halves(tiles[slot].T)
    for copy in copies[:3]:
        copy.wait()
    for slot in range(slots):
        guide[0, slot] = spots[0, slot]
        guide[1, slot] = spots[1, slot]
    guide[4, 0] = live[0, 0]


def prepare(groups, *arrays):
    slots = arrays[-1].shape[0]
    width = max(slots, groups)
    held = [jax.ShapeDtypeStruct(x.shape, x.dtype) for x in arrays[2:]]
    half = jax.ShapeDtypeStruct(arrays[-1].shape, bf16)
    return pl.pallas_call(
        functools.partial(prepare_kernel, groups),
        out_shape=(pltpu.SMEM((5, width), jnp.int32), *held, half, half),
        in_specs=[hbm, vmem, hbm, hbm],
        out_specs=(smem,) + (vmem,) * 4,
        scratch_shapes=[
            pltpu.SMEM(arrays[0].shape, jnp.int32),
            pltpu.SMEM(arrays[1].shape, jnp.int32),
            pltpu.SemaphoreType.DMA((slots + 3,)),
        ],
        compiler_params=room,
        name="prepare",
    )(*[x if i == 1 else pltpu.with_memory_space_constraint(x, pltpu.HBM) for i, x in enumerate(arrays)])


def partial_kernel(guide, samples, diag, high, low, *refs):
    pieces = refs[:-4]
    groups = 2 * len(pieces)
    kept, sent, panel, total = refs[-4:]
    col = lax.axis_index("col")
    rep = lax.axis_index("rep")
    rows = samples.shape[1]
    for turn, piece in enumerate(pieces):
        for half in range(2):
            block = guide[2, turn] ^ half
            panel[block, :rows], panel[block, rows:] = halves(piece[half])
    total[...] = jnp.zeros_like(total)

    def term(x_high, both, w_high, w_low):
        wide = dot(both, w_high)
        return wide[:rows] + wide[rows:] + dot(x_high, w_low)

    own_high, own_low = halves(samples[0])
    total[col * 2 + rep] = term(
        own_high, jnp.concatenate([own_high, own_low], axis=0), *halves(diag[0])
    )
    for slot in range(high.shape[0]):
        source = panel.at[guide[1, slot]]
        value = term(source[:rows], source[...], high[slot], low[slot])
        total[guide[0, slot]] += jnp.where(slot < guide[4, 0], value, 0.0)
    for pair in range(groups // 2):
        kept[pair] = total[2 * pair + rep]
        sent[pair] = total[2 * pair + 1 - rep]


def partial_image(guide, samples, diag, high, low, pieces):
    groups = 2 * len(pieces)
    _, rows, side = samples.shape
    half = jax.ShapeDtypeStruct((groups // 2, rows, side), f32)
    panel = jax.ShapeDtypeStruct((groups, 2 * rows, side), bf16)
    return pl.pallas_call(
        partial_kernel,
        out_shape=(half, half, panel),
        in_specs=[smem] + [vmem] * (4 + len(pieces)),
        out_specs=(vmem, vmem, vmem),
        scratch_shapes=[pltpu.VMEM((groups, rows, side), f32)],
        compiler_params=room,
        name="partial_image",
    )(guide, samples, diag, high, low, *pieces)


def half_gradient_kernel(
    guide, own_image, other_image, samples, panel, diag, tiles, moved, new_diag, wide, low, step, sem
):
    pairs, rows, side = own_image.shape
    rep = lax.axis_index("rep")
    left_high, left_low = halves(samples[0].T)
    right_high, right_low = halves(own_image[lax.axis_index("col")])
    one_side = dot(left_high, right_high) + dot(left_low, right_high) + dot(left_high, right_low)
    tile = diag[0]
    line = lax.broadcasted_iota(jnp.int32, (side, side), 0)
    on_diag = line == lax.broadcasted_iota(jnp.int32, (side, side), 1)
    scale = step_size / (2.0 * rows)
    shifted = tile - (one_side + one_side.T) * scale
    inverse = step_size / jnp.where(on_diag, tile, 1.0)
    step[0] = jnp.where(on_diag, shifted + inverse, soft_limit(shifted))
    copy = pltpu.make_async_copy(step, new_diag, sem)
    copy.start()
    for pair in range(pairs):
        for parity, image in ((rep, own_image), (1 - rep, other_image)):
            block = 2 * pair + parity
            image_high, low[block] = halves(image[pair].T)
            wide[block, :, :rows] = image_high
            wide[block, :, rows:] = image_high
    for slot in range(tiles.shape[0]):
        left, right = guide[0, slot], guide[1, slot]
        gradient = dot(wide[left], panel[right]) + dot(low[left], panel[right, :rows])
        moved[slot] = tiles[slot] - gradient * scale
    copy.wait()


def half_gradient(guide, own_image, other_image, samples, panel, diag, tiles):
    groups, _, side = panel.shape
    rows = samples.shape[1]
    return pl.pallas_call(
        half_gradient_kernel,
        out_shape=(
            jax.ShapeDtypeStruct(tiles.shape, f32),
            jax.ShapeDtypeStruct(diag.shape, f32),
        ),
        in_specs=[smem] + [vmem] * 6,
        out_specs=(vmem, hbm),
        scratch_shapes=[
            pltpu.VMEM((groups, side, 2 * rows), bf16),
            pltpu.VMEM((groups, side, rows), bf16),
            pltpu.VMEM(diag.shape, f32),
            pltpu.SemaphoreType.DMA,
        ],
        compiler_params=room,
        name="half_gradient",
    )(guide, own_image, other_image, samples, panel, diag, tiles)


def row_panel_kernel(*refs):
    samples, (wide, low) = refs[:-2], refs[-2:]
    rep = lax.axis_index("rep")
    col = lax.axis_index("col")
    rows = samples[0].shape[1]
    pairs = len(samples)
    for turn, piece in enumerate(samples):
        line = 2 * lax.rem(col + pairs - turn, pairs)
        for block, place in ((line + rep, 0), (line + 1 - rep, 1)):
            high, low[block] = halves(piece[place].T)
            wide[block, :, :rows] = high
            wide[block, :, rows:] = high


def row_panel(samples):
    _, rows, side = samples[0].shape
    groups = 2 * len(samples)
    return pl.pallas_call(
        row_panel_kernel,
        out_shape=(
            jax.ShapeDtypeStruct((groups, side, 2 * rows), bf16),
            jax.ShapeDtypeStruct((groups, side, rows), bf16),
        ),
        in_specs=[vmem] * len(samples),
        out_specs=(vmem, vmem),
        compiler_params=room,
        name="row_panel",
    )(*samples)


def slots_kernel(guide, wide, low, first, second, moved, out, panel, ready, sems):
    pairs, rows, _ = first.shape
    for pair in range(pairs):
        for turn, piece in enumerate((first, second)):
            block = 2 * pair + guide[3, turn]
            panel[block, :rows], panel[block, rows:] = halves(piece[pair])
    copies = []
    for slot in range(moved.shape[0]):
        left, right = guide[0, slot], guide[1, slot]
        gradient = dot(wide[left], panel[right]) + dot(low[left], panel[right, :rows])
        value = soft_limit(moved[slot] - gradient * (step_size / (2.0 * rows)))
        ready[slot] = jnp.where(slot < guide[4, 0], value, 0.0)
        copies.append(pltpu.make_async_copy(ready.at[slot], out.at[slot], sems.at[slot]))
        copies[-1].start()
    for copy in copies:
        copy.wait()


def update_slots(guide, wide, low, first, second, moved):
    slots, side, _ = moved.shape
    groups, _, depth = wide.shape
    return pl.pallas_call(
        slots_kernel,
        out_shape=jax.ShapeDtypeStruct(moved.shape, f32),
        in_specs=[smem] + [vmem] * 5,
        out_specs=hbm,
        scratch_shapes=[
            pltpu.VMEM((groups, depth, side), bf16),
            pltpu.VMEM(moved.shape, f32),
            pltpu.SemaphoreType.DMA((slots,)),
        ],
        compiler_params=room,
        name="update_slots",
    )(guide, wide, low, first, second, moved)


def on_device(samples, diag_tiles, omega_slots, tile_pos, tile_count):
    groups = lax.axis_size(line_axes)
    cols = lax.axis_size("col")
    slots, side = omega_slots.shape[2], omega_slots.shape[3]
    tiles = omega_slots.reshape(slots, side, side)
    place = tile_pos.reshape(slots, 2).T
    span = range(groups)

    def links(source, turn):
        return [
            (line * groups + source(turn, row, line, groups), row * groups + line)
            for line in span
            for row in span
        ]

    def around(size, turn):
        return [(j, (j + turn) % size) for j in range(size)]

    first = samples[None]
    pair = lax.dynamic_update_slice(jnp.zeros((2, *samples.shape), f32), first, (0, 0, 0))
    pair = lax.optimization_barrier(pair)
    pair = lax.dynamic_update_slice(
        pair, lax.ppermute(first, "rep", around(2, 1)), (1, 0, 0)
    )
    col_pieces = [
        lax.ppermute(pair, grid_axes, links(sample_source, turn)) for turn in range(cols)
    ]
    guide, own_diag, held, high, low = prepare(groups, place, tile_count, diag_tiles, tiles)
    kept, sent, panel = partial_image(guide, pair, own_diag, high, low, col_pieces)
    chip = kept + lax.ppermute(sent, "rep", around(2, 1))
    image = chip
    for turn in range(1, cols):
        image = image + lax.ppermute(chip, "col", around(cols, turn))

    late, image = lax.optimization_barrier((pair, image))
    beside = [lax.ppermute(late, "col", around(cols, turn)) for turn in range(1, cols)]
    first, second = [
        lax.ppermute(image, grid_axes, links(image_source, turn)) for turn in range(2)
    ]
    other = lax.ppermute(image, "rep", around(2, 1))
    moved, new_diag = half_gradient(guide, image, other, pair, panel, own_diag, held)
    wide, low = row_panel([pair, *beside])
    new_slots = update_slots(guide, wide, low, first, second, moved)
    return new_slots.reshape(omega_slots.shape), new_diag


def solution(mesh):
    placed = (
        P("parts", ("row", "col", "rep")),
        P(("parts", "row", "col", "rep"), None, None),
        P(("parts", "row"), ("col", "rep"), None, None, None),
        P(("parts", "row"), ("col", "rep"), None, None),
        P(("parts", "row"), ("col", "rep")),
    )
    return jax.shard_map(
        on_device,
        mesh=mesh,
        in_specs=placed,
        out_specs=(
            P(("parts", "row"), ("col", "rep"), None, None, None),
            P(("parts", "row", "col", "rep"), None, None),
        ),
        check_vma=False,
    )
```

```python
import functools

import jax
import jax.numpy as jnp
from jax import lax
from jax.experimental import pallas as pl
from jax.experimental.pallas import tpu as pltpu
from jax.sharding import PartitionSpec as P

step_size = 1.0
penalty = 0.1
grid_axes = ("row", "col", "rep")
line_axes = ("col", "rep")
f32 = jnp.float32
bf16 = jnp.bfloat16
vmem = pl.BlockSpec(memory_space=pltpu.VMEM)
smem = pl.BlockSpec(memory_space=pltpu.SMEM)
hbm = pl.BlockSpec(memory_space=pltpu.HBM)
room = pltpu.CompilerParams(vmem_limit_bytes=24 * 2**20)


def halves(values):
    high = values.astype(bf16)
    return high, (values - high.astype(f32)).astype(bf16)


def dot(left, right):
    return jnp.dot(left, right, preferred_element_type=f32)


def soft_limit(values):
    limit_value = step_size * penalty
    return values - jnp.clip(values, -limit_value, limit_value)


def first_source(row, own, groups):
    rep = (row // 2 ^ row ^ own // (groups // 2)) & 1
    return 2 * (row // 2 ^ rep) + rep


def sample_source(turn, row, own, groups):
    spot = groups // 2 - 1 - turn
    return first_source(row, own, groups) ^ (2 * spot + spot % 2)


def image_source(turn, row, own, groups):
    return first_source(row, own, groups) ^ ((1 - turn) * (groups - 1))


def prepare_kernel(groups, *refs):
    place, count, *arrays = refs[:4]
    guide, *held, high, low, spots, live, sems = refs[4:]
    tiles = held[1]
    slots = tiles.shape[0]
    pairs = [(place, spots), (count, live), (arrays[0], held[0])]
    pairs += [(arrays[1].at[slot], tiles.at[slot]) for slot in range(slots)]
    copies = [pltpu.make_async_copy(*pair, sems.at[i]) for i, pair in enumerate(pairs)]
    for copy in copies:
        copy.start()
    row = lax.axis_index("row")
    own = lax.axis_index("col") * 2 + lax.axis_index("rep")
    for turn in range(groups // 2):
        guide[2, turn] = sample_source(turn, row, own, groups)
    for turn in range(2):
        guide[3, turn] = image_source(turn, row, own, groups) & 1
    for slot in range(slots):
        copies[3 + slot].wait()
        high[slot], low[slot] = halves(tiles[slot].T)
    for copy in copies[:3]:
        copy.wait()
    for slot in range(slots):
        guide[0, slot] = spots[0, slot]
        guide[1, slot] = spots[1, slot]
    guide[4, 0] = live[0, 0]


def prepare(groups, *arrays):
    slots = arrays[-1].shape[0]
    width = max(slots, groups)
    held = [jax.ShapeDtypeStruct(x.shape, x.dtype) for x in arrays[2:]]
    half = jax.ShapeDtypeStruct(arrays[-1].shape, bf16)
    return pl.pallas_call(
        functools.partial(prepare_kernel, groups),
        out_shape=(pltpu.SMEM((5, width), jnp.int32), *held, half, half),
        in_specs=[hbm, vmem, hbm, hbm],
        out_specs=(smem,) + (vmem,) * 4,
        scratch_shapes=[
            pltpu.SMEM(arrays[0].shape, jnp.int32),
            pltpu.SMEM(arrays[1].shape, jnp.int32),
            pltpu.SemaphoreType.DMA((slots + 3,)),
        ],
        compiler_params=room,
        name="prepare",
    )(*[x if i == 1 else pltpu.with_memory_space_constraint(x, pltpu.HBM) for i, x in enumerate(arrays)])


def partial_kernel(guide, samples, diag, high, low, *refs):
    pieces = refs[:-4]
    groups = 2 * len(pieces)
    kept, sent, panel, total = refs[-4:]
    col = lax.axis_index("col")
    rep = lax.axis_index("rep")
    rows = samples.shape[1]
    for turn, piece in enumerate(pieces):
        for half in range(2):
            block = guide[2, turn] ^ half
            panel[block, :rows], panel[block, rows:] = halves(piece[half])
    total[...] = jnp.zeros_like(total)

    def term(x_high, both, w_high, w_low):
        wide = dot(both, w_high)
        return wide[:rows] + wide[rows:] + dot(x_high, w_low)

    own_high, own_low = halves(samples[0])
    total[col * 2 + rep] = term(
        own_high, jnp.concatenate([own_high, own_low], axis=0), *halves(diag[0])
    )
    for slot in range(high.shape[0]):
        source = panel.at[guide[1, slot]]
        value = term(source[:rows], source[...], high[slot], low[slot])
        total[guide[0, slot]] += jnp.where(slot < guide[4, 0], value, 0.0)
    for pair in range(groups // 2):
        kept[pair] = total[2 * pair + rep]
        sent[pair] = total[2 * pair + 1 - rep]


def partial_image(guide, samples, diag, high, low, pieces):
    groups = 2 * len(pieces)
    _, rows, side = samples.shape
    half = jax.ShapeDtypeStruct((groups // 2, rows, side), f32)
    panel = jax.ShapeDtypeStruct((groups, 2 * rows, side), bf16)
    return pl.pallas_call(
        partial_kernel,
        out_shape=(half, half, panel),
        in_specs=[smem] + [vmem] * (4 + len(pieces)),
        out_specs=(vmem, vmem, vmem),
        scratch_shapes=[pltpu.VMEM((groups, rows, side), f32)],
        compiler_params=room,
        name="partial_image",
    )(guide, samples, diag, high, low, *pieces)


def half_gradient_kernel(
    guide, own_image, other_image, samples, panel, diag, tiles, moved, new_diag, wide, low, step, sem
):
    pairs, rows, side = own_image.shape
    rep = lax.axis_index("rep")
    left_high, left_low = halves(samples[0].T)
    right_high, right_low = halves(own_image[lax.axis_index("col")])
    one_side = dot(left_high, right_high) + dot(left_low, right_high) + dot(left_high, right_low)
    tile = diag[0]
    line = lax.broadcasted_iota(jnp.int32, (side, side), 0)
    on_diag = line == lax.broadcasted_iota(jnp.int32, (side, side), 1)
    scale = step_size / (2.0 * rows)
    shifted = tile - (one_side + one_side.T) * scale
    inverse = step_size / jnp.where(on_diag, tile, 1.0)
    step[0] = jnp.where(on_diag, shifted + inverse, soft_limit(shifted))
    copy = pltpu.make_async_copy(step, new_diag, sem)
    copy.start()
    for pair in range(pairs):
        for parity, image in ((rep, own_image), (1 - rep, other_image)):
            block = 2 * pair + parity
            image_high, low[block] = halves(image[pair].T)
            wide[block, :, :rows] = image_high
            wide[block, :, rows:] = image_high
    for slot in range(tiles.shape[0]):
        left, right = guide[0, slot], guide[1, slot]
        gradient = dot(wide[left], panel[right]) + dot(low[left], panel[right, :rows])
        moved[slot] = tiles[slot] - gradient * scale
    copy.wait()


def half_gradient(guide, own_image, other_image, samples, panel, diag, tiles):
    groups, _, side = panel.shape
    rows = samples.shape[1]
    return pl.pallas_call(
        half_gradient_kernel,
        out_shape=(
            jax.ShapeDtypeStruct(tiles.shape, f32),
            jax.ShapeDtypeStruct(diag.shape, f32),
        ),
        in_specs=[smem] + [vmem] * 6,
        out_specs=(vmem, hbm),
        scratch_shapes=[
            pltpu.VMEM((groups, side, 2 * rows), bf16),
            pltpu.VMEM((groups, side, rows), bf16),
            pltpu.VMEM(diag.shape, f32),
            pltpu.SemaphoreType.DMA,
        ],
        compiler_params=room,
        name="half_gradient",
    )(guide, own_image, other_image, samples, panel, diag, tiles)


def row_panel_kernel(*refs):
    samples, (wide, low) = refs[:-2], refs[-2:]
    rep = lax.axis_index("rep")
    col = lax.axis_index("col")
    rows = samples[0].shape[1]
    pairs = len(samples)
    for turn, piece in enumerate(samples):
        line = 2 * lax.rem(col + pairs - turn, pairs)
        for block, place in ((line + rep, 0), (line + 1 - rep, 1)):
            high, low[block] = halves(piece[place].T)
            wide[block, :, :rows] = high
            wide[block, :, rows:] = high


def row_panel(samples):
    _, rows, side = samples[0].shape
    groups = 2 * len(samples)
    return pl.pallas_call(
        row_panel_kernel,
        out_shape=(
            jax.ShapeDtypeStruct((groups, side, 2 * rows), bf16),
            jax.ShapeDtypeStruct((groups, side, rows), bf16),
        ),
        in_specs=[vmem] * len(samples),
        out_specs=(vmem, vmem),
        compiler_params=room,
        name="row_panel",
    )(*samples)


def slots_kernel(guide, wide, low, first, second, moved, out, panel, ready, sems):
    pairs, rows, _ = first.shape
    for pair in range(pairs):
        for turn, piece in enumerate((first, second)):
            block = 2 * pair + guide[3, turn]
            panel[block, :rows], panel[block, rows:] = halves(piece[pair])
    copies = []
    for slot in range(moved.shape[0]):
        left, right = guide[0, slot], guide[1, slot]
        gradient = dot(wide[left], panel[right]) + dot(low[left], panel[right, :rows])
        value = soft_limit(moved[slot] - gradient * (step_size / (2.0 * rows)))
        ready[slot] = jnp.where(slot < guide[4, 0], value, 0.0)
        copies.append(pltpu.make_async_copy(ready.at[slot], out.at[slot], sems.at[slot]))
        copies[-1].start()
    for copy in copies:
        copy.wait()


def update_slots(guide, wide, low, first, second, moved):
    slots, side, _ = moved.shape
    groups, _, depth = wide.shape
    return pl.pallas_call(
        slots_kernel,
        out_shape=jax.ShapeDtypeStruct(moved.shape, f32),
        in_specs=[smem] + [vmem] * 5,
        out_specs=hbm,
        scratch_shapes=[
            pltpu.VMEM((groups, depth, side), bf16),
            pltpu.VMEM(moved.shape, f32),
            pltpu.SemaphoreType.DMA((slots,)),
        ],
        compiler_params=room,
        name="update_slots",
    )(guide, wide, low, first, second, moved)


def on_device(samples, diag_tiles, omega_slots, tile_pos, tile_count):
    groups = lax.axis_size(line_axes)
    cols = lax.axis_size("col")
    slots, side = omega_slots.shape[2], omega_slots.shape[3]
    tiles = omega_slots.reshape(slots, side, side)
    place = tile_pos.reshape(slots, 2).T
    span = range(groups)

    def links(source, turn):
        return [
            (line * groups + source(turn, row, line, groups), row * groups + line)
            for line in span
            for row in span
        ]

    def around(size, turn):
        return [(j, (j + turn) % size) for j in range(size)]

    first = samples[None]
    pair = lax.dynamic_update_slice(jnp.zeros((2, *samples.shape), f32), first, (0, 0, 0))
    pair = lax.optimization_barrier(pair)
    pair = lax.dynamic_update_slice(
        pair, lax.ppermute(first, "rep", around(2, 1)), (1, 0, 0)
    )
    col_pieces = [
        lax.ppermute(pair, grid_axes, links(sample_source, turn)) for turn in range(cols)
    ]
    guide, own_diag, held, high, low = prepare(groups, place, tile_count, diag_tiles, tiles)
    kept, sent, panel = partial_image(guide, pair, own_diag, high, low, col_pieces)
    chip = kept + lax.ppermute(sent, "rep", around(2, 1))
    image = chip
    for turn in range(1, cols):
        image = image + lax.ppermute(chip, "col", around(cols, turn))

    late, image = lax.optimization_barrier((pair, image))
    beside = [lax.ppermute(late, "col", around(cols, turn)) for turn in range(1, cols)]
    first, second = [
        lax.ppermute(image, grid_axes, links(image_source, turn)) for turn in range(2)
    ]
    other = lax.ppermute(image, "rep", around(2, 1))
    moved, new_diag = half_gradient(guide, image, other, pair, panel, own_diag, held)
    beside, moved = lax.optimization_barrier((beside, moved))
    wide, low = row_panel([pair, *beside])
    new_slots = update_slots(guide, wide, low, first, second, moved)
    return new_slots.reshape(omega_slots.shape), new_diag


def solution(mesh):
    placed = (
        P("parts", ("row", "col", "rep")),
        P(("parts", "row", "col", "rep"), None, None),
        P(("parts", "row"), ("col", "rep"), None, None, None),
        P(("parts", "row"), ("col", "rep"), None, None),
        P(("parts", "row"), ("col", "rep")),
    )
    return jax.shard_map(
        on_device,
        mesh=mesh,
        in_specs=placed,
        out_specs=(
            P(("parts", "row"), ("col", "rep"), None, None, None),
            P(("parts", "row", "col", "rep"), None, None),
        ),
        check_vma=False,
    )
```

```python
import functools

import jax
import jax.numpy as jnp
from jax import lax
from jax.experimental import pallas as pl
from jax.experimental.pallas import tpu as pltpu
from jax.sharding import PartitionSpec as P

step_size = 1.0
penalty = 0.1
grid_axes = ("row", "col", "rep")
line_axes = ("col", "rep")
f32 = jnp.float32
bf16 = jnp.bfloat16
vmem = pl.BlockSpec(memory_space=pltpu.VMEM)
smem = pl.BlockSpec(memory_space=pltpu.SMEM)
hbm = pl.BlockSpec(memory_space=pltpu.HBM)
room = pltpu.CompilerParams(vmem_limit_bytes=24 * 2**20)


def halves(values):
    high = values.astype(bf16)
    return high, (values - high.astype(f32)).astype(bf16)


def dot(left, right):
    return jnp.dot(left, right, preferred_element_type=f32)


def soft_limit(values):
    limit_value = step_size * penalty
    return values - jnp.clip(values, -limit_value, limit_value)


def first_source(row, own, groups):
    rep = (row // 2 ^ row ^ own // (groups // 2)) & 1
    return 2 * (row // 2 ^ rep) + rep


def sample_source(turn, row, own, groups):
    spot = groups // 2 - 1 - turn
    return first_source(row, own, groups) ^ (2 * spot + spot % 2)


def image_source(turn, row, own, groups):
    return first_source(row, own, groups) ^ ((1 - turn) * (groups - 1))


def prepare_kernel(groups, *refs):
    place, count, *arrays = refs[:4]
    guide, *held, high, low, spots, live, sems = refs[4:]
    tiles = held[1]
    slots = tiles.shape[0]
    pairs = [(place, spots), (count, live), (arrays[0], held[0])]
    pairs += [(arrays[1].at[slot], tiles.at[slot]) for slot in range(slots)]
    copies = [pltpu.make_async_copy(*pair, sems.at[i]) for i, pair in enumerate(pairs)]
    for copy in copies:
        copy.start()
    row = lax.axis_index("row")
    own = lax.axis_index("col") * 2 + lax.axis_index("rep")
    for turn in range(groups // 2):
        guide[2, turn] = sample_source(turn, row, own, groups)
    for turn in range(2):
        guide[3, turn] = image_source(turn, row, own, groups) & 1
    for slot in range(slots):
        copies[3 + slot].wait()
        high[slot], low[slot] = halves(tiles[slot].T)
    for copy in copies[:3]:
        copy.wait()
    for slot in range(slots):
        guide[0, slot] = spots[0, slot]
        guide[1, slot] = spots[1, slot]
    guide[4, 0] = live[0, 0]


def prepare(groups, *arrays):
    slots = arrays[-1].shape[0]
    width = max(slots, groups)
    held = [jax.ShapeDtypeStruct(x.shape, x.dtype) for x in arrays[2:]]
    half = jax.ShapeDtypeStruct(arrays[-1].shape, bf16)
    return pl.pallas_call(
        functools.partial(prepare_kernel, groups),
        out_shape=(pltpu.SMEM((5, width), jnp.int32), *held, half, half),
        in_specs=[hbm, vmem, hbm, hbm],
        out_specs=(smem,) + (vmem,) * 4,
        scratch_shapes=[
            pltpu.SMEM(arrays[0].shape, jnp.int32),
            pltpu.SMEM(arrays[1].shape, jnp.int32),
            pltpu.SemaphoreType.DMA((slots + 3,)),
        ],
        compiler_params=room,
        name="prepare",
    )(*[x if i == 1 else pltpu.with_memory_space_constraint(x, pltpu.HBM) for i, x in enumerate(arrays)])


def partial_kernel(guide, samples, diag, high, low, *refs):
    pieces = refs[:-4]
    groups = 2 * len(pieces)
    kept, sent, panel, total = refs[-4:]
    col = lax.axis_index("col")
    rep = lax.axis_index("rep")
    rows = samples.shape[1]
    for turn, piece in enumerate(pieces):
        for half in range(2):
            block = guide[2, turn] ^ half
            panel[block, :rows], panel[block, rows:] = halves(piece[half])
    total[...] = jnp.zeros_like(total)

    def term(x_high, both, w_high, w_low):
        wide = dot(both, w_high)
        return wide[:rows] + wide[rows:] + dot(x_high, w_low)

    own_high, own_low = halves(samples[0])
    total[col * 2 + rep] = term(
        own_high, jnp.concatenate([own_high, own_low], axis=0), *halves(diag[0])
    )
    for slot in range(high.shape[0]):
        source = panel.at[guide[1, slot]]
        value = term(source[:rows], source[...], high[slot], low[slot])
        total[guide[0, slot]] += jnp.where(slot < guide[4, 0], value, 0.0)
    for pair in range(groups // 2):
        kept[pair] = total[2 * pair + rep]
        sent[pair] = total[2 * pair + 1 - rep]


def partial_image(guide, samples, diag, high, low, pieces):
    groups = 2 * len(pieces)
    _, rows, side = samples.shape
    half = jax.ShapeDtypeStruct((groups // 2, rows, side), f32)
    panel = jax.ShapeDtypeStruct((groups, 2 * rows, side), bf16)
    return pl.pallas_call(
        partial_kernel,
        out_shape=(half, half, panel),
        in_specs=[smem] + [vmem] * (4 + len(pieces)),
        out_specs=(vmem, vmem, vmem),
        scratch_shapes=[pltpu.VMEM((groups, rows, side), f32)],
        compiler_params=room,
        name="partial_image",
    )(guide, samples, diag, high, low, *pieces)


def half_gradient_kernel(
    guide, own_image, other_image, samples, panel, diag, tiles, moved, new_diag, wide, low, step, sem
):
    pairs, rows, side = own_image.shape
    rep = lax.axis_index("rep")
    left_high, left_low = halves(samples[0].T)
    right_high, right_low = halves(own_image[lax.axis_index("col")])
    one_side = dot(left_high, right_high) + dot(left_low, right_high) + dot(left_high, right_low)
    tile = diag[0]
    line = lax.broadcasted_iota(jnp.int32, (side, side), 0)
    on_diag = line == lax.broadcasted_iota(jnp.int32, (side, side), 1)
    scale = step_size / (2.0 * rows)
    shifted = tile - (one_side + one_side.T) * scale
    inverse = step_size / jnp.where(on_diag, tile, 1.0)
    step[0] = jnp.where(on_diag, shifted + inverse, soft_limit(shifted))
    copy = pltpu.make_async_copy(step, new_diag, sem)
    copy.start()
    for pair in range(pairs):
        for parity, image in ((rep, own_image), (1 - rep, other_image)):
            block = 2 * pair + parity
            image_high, low[block] = halves(image[pair].T)
            wide[block, :, :rows] = image_high
            wide[block, :, rows:] = image_high
    for slot in range(tiles.shape[0]):
        left, right = guide[0, slot], guide[1, slot]
        gradient = dot(wide[left], panel[right]) + dot(low[left], panel[right, :rows])
        moved[slot] = tiles[slot] - gradient * scale
    copy.wait()


def half_gradient(guide, own_image, other_image, samples, panel, diag, tiles):
    groups, _, side = panel.shape
    rows = samples.shape[1]
    return pl.pallas_call(
        half_gradient_kernel,
        out_shape=(
            jax.ShapeDtypeStruct(tiles.shape, f32),
            jax.ShapeDtypeStruct(diag.shape, f32),
        ),
        in_specs=[smem] + [vmem] * 6,
        out_specs=(vmem, hbm),
        scratch_shapes=[
            pltpu.VMEM((groups, side, 2 * rows), bf16),
            pltpu.VMEM((groups, side, rows), bf16),
            pltpu.VMEM(diag.shape, f32),
            pltpu.SemaphoreType.DMA,
        ],
        compiler_params=room,
        name="half_gradient",
    )(guide, own_image, other_image, samples, panel, diag, tiles)


def row_panel_kernel(pair, *refs):
    pieces, (wide, low) = refs[:-2], refs[-2:]
    rep = lax.axis_index("rep")
    col = lax.axis_index("col")
    pairs, rows = len(pieces) // 2 + 1, pair.shape[1]
    lines = [(pair[0], pair[1])]
    lines += [(pieces[k][...], pieces[k + pairs - 1][...]) for k in range(pairs - 1)]
    for turn, (same, other) in enumerate(lines):
        line = 2 * lax.rem(col + pairs - turn, pairs)
        for block, values in ((line + rep, same), (line + 1 - rep, other)):
            high, low[block] = halves(values.T)
            wide[block, :, :rows] = high
            wide[block, :, rows:] = high


def row_panel(pair, pieces):
    _, rows, side = pair.shape
    groups = len(pieces) + 2
    return pl.pallas_call(
        row_panel_kernel,
        out_shape=(
            jax.ShapeDtypeStruct((groups, side, 2 * rows), bf16),
            jax.ShapeDtypeStruct((groups, side, rows), bf16),
        ),
        in_specs=[vmem] * (1 + len(pieces)),
        out_specs=(vmem, vmem),
        compiler_params=room,
        name="row_panel",
    )(pair, *pieces)


def slots_kernel(guide, wide, low, first, second, moved, out, panel, ready, sems):
    pairs, rows, _ = first.shape
    for pair in range(pairs):
        for turn, piece in enumerate((first, second)):
            block = 2 * pair + guide[3, turn]
            panel[block, :rows], panel[block, rows:] = halves(piece[pair])
    copies = []
    for slot in range(moved.shape[0]):
        left, right = guide[0, slot], guide[1, slot]
        gradient = dot(wide[left], panel[right]) + dot(low[left], panel[right, :rows])
        value = soft_limit(moved[slot] - gradient * (step_size / (2.0 * rows)))
        ready[slot] = jnp.where(slot < guide[4, 0], value, 0.0)
        copies.append(pltpu.make_async_copy(ready.at[slot], out.at[slot], sems.at[slot]))
        copies[-1].start()
    for copy in copies:
        copy.wait()


def update_slots(guide, wide, low, first, second, moved):
    slots, side, _ = moved.shape
    groups, _, depth = wide.shape
    return pl.pallas_call(
        slots_kernel,
        out_shape=jax.ShapeDtypeStruct(moved.shape, f32),
        in_specs=[smem] + [vmem] * 5,
        out_specs=hbm,
        scratch_shapes=[
            pltpu.VMEM((groups, depth, side), bf16),
            pltpu.VMEM(moved.shape, f32),
            pltpu.SemaphoreType.DMA((slots,)),
        ],
        compiler_params=room,
        name="update_slots",
    )(guide, wide, low, first, second, moved)


def on_device(samples, diag_tiles, omega_slots, tile_pos, tile_count):
    groups = lax.axis_size(line_axes)
    cols = lax.axis_size("col")
    slots, side = omega_slots.shape[2], omega_slots.shape[3]
    tiles = omega_slots.reshape(slots, side, side)
    place = tile_pos.reshape(slots, 2).T
    span = range(groups)

    def links(source, turn):
        return [
            (line * groups + source(turn, row, line, groups), row * groups + line)
            for line in span
            for row in span
        ]

    def around(size, turn):
        return [(j, (j + turn) % size) for j in range(size)]

    first = samples[None]
    pair = lax.dynamic_update_slice(jnp.zeros((2, *samples.shape), f32), first, (0, 0, 0))
    pair = lax.optimization_barrier(pair)
    pair = lax.dynamic_update_slice(
        pair, lax.ppermute(first, "rep", around(2, 1)), (1, 0, 0)
    )
    col_pieces = [
        lax.ppermute(pair, grid_axes, links(sample_source, turn)) for turn in range(cols)
    ]
    guide, own_diag, held, high, low = prepare(groups, place, tile_count, diag_tiles, tiles)
    kept, sent, panel = partial_image(guide, pair, own_diag, high, low, col_pieces)
    chip = kept + lax.ppermute(sent, "rep", around(2, 1))
    image = chip
    for turn in range(1, cols):
        image = image + lax.ppermute(chip, "col", around(cols, turn))

    samples_late, image = lax.optimization_barrier((samples, image))
    beside = [lax.ppermute(samples_late, "col", around(cols, turn)) for turn in range(1, cols)]
    across = [lax.ppermute(block, "rep", around(2, 1)) for block in beside]
    first, second = [
        lax.ppermute(image, grid_axes, links(image_source, turn)) for turn in range(2)
    ]
    other = lax.ppermute(image, "rep", around(2, 1))
    moved, new_diag = half_gradient(guide, image, other, pair, panel, own_diag, held)
    beside, moved = lax.optimization_barrier((beside + across, moved))
    wide, low = row_panel(pair, beside)
    new_slots = update_slots(guide, wide, low, first, second, moved)
    return new_slots.reshape(omega_slots.shape), new_diag


def solution(mesh):
    placed = (
        P("parts", ("row", "col", "rep")),
        P(("parts", "row", "col", "rep"), None, None),
        P(("parts", "row"), ("col", "rep"), None, None, None),
        P(("parts", "row"), ("col", "rep"), None, None),
        P(("parts", "row"), ("col", "rep")),
    )
    return jax.shard_map(
        on_device,
        mesh=mesh,
        in_specs=placed,
        out_specs=(
            P(("parts", "row"), ("col", "rep"), None, None, None),
            P(("parts", "row", "col", "rep"), None, None),
        ),
        check_vma=False,
    )
```

```python
import functools

import jax
import jax.numpy as jnp
from jax import lax
from jax.experimental import pallas as pl
from jax.experimental.pallas import tpu as pltpu
from jax.sharding import PartitionSpec as P

step_size = 1.0
penalty = 0.1
grid_axes = ("row", "col", "rep")
line_axes = ("col", "rep")
f32 = jnp.float32
bf16 = jnp.bfloat16
vmem = pl.BlockSpec(memory_space=pltpu.VMEM)
smem = pl.BlockSpec(memory_space=pltpu.SMEM)
hbm = pl.BlockSpec(memory_space=pltpu.HBM)
room = pltpu.CompilerParams(vmem_limit_bytes=24 * 2**20)


def halves(values):
    high = values.astype(bf16)
    return high, (values - high.astype(f32)).astype(bf16)


def dot(left, right):
    return jnp.dot(left, right, preferred_element_type=f32)


def soft_limit(values):
    limit_value = step_size * penalty
    return values - jnp.clip(values, -limit_value, limit_value)


def first_source(row, own, groups):
    rep = (row // 2 ^ row ^ own // (groups // 2)) & 1
    return 2 * (row // 2 ^ rep) + rep


def sample_source(turn, row, own, groups):
    return first_source(row, own, groups) ^ (2 * turn + turn % 2)


def image_source(turn, row, own, groups):
    return first_source(row, own, groups) ^ ((1 - turn) * (groups - 1))


def prepare_kernel(groups, *refs):
    place, count, *arrays = refs[:4]
    guide, *held, high, low, spots, live, sems = refs[4:]
    tiles = held[1]
    slots = tiles.shape[0]
    pairs = [(place, spots), (count, live), (arrays[0], held[0])]
    pairs += [(arrays[1].at[slot], tiles.at[slot]) for slot in range(slots)]
    copies = [pltpu.make_async_copy(*pair, sems.at[i]) for i, pair in enumerate(pairs)]
    for copy in copies:
        copy.start()
    row = lax.axis_index("row")
    own = lax.axis_index("col") * 2 + lax.axis_index("rep")
    for turn in range(groups // 2):
        guide[2, turn] = sample_source(turn, row, own, groups)
    for turn in range(2):
        guide[3, turn] = image_source(turn, row, own, groups) & 1
    for slot in range(slots):
        copies[3 + slot].wait()
        high[slot], low[slot] = halves(tiles[slot].T)
    for copy in copies[:3]:
        copy.wait()
    for slot in range(slots):
        guide[0, slot] = spots[0, slot]
        guide[1, slot] = spots[1, slot]
    guide[4, 0] = live[0, 0]


def prepare(groups, *arrays):
    slots = arrays[-1].shape[0]
    width = max(slots, groups)
    held = [jax.ShapeDtypeStruct(x.shape, x.dtype) for x in arrays[2:]]
    half = jax.ShapeDtypeStruct(arrays[-1].shape, bf16)
    return pl.pallas_call(
        functools.partial(prepare_kernel, groups),
        out_shape=(pltpu.SMEM((5, width), jnp.int32), *held, half, half),
        in_specs=[hbm, vmem, hbm, hbm],
        out_specs=(smem,) + (vmem,) * 4,
        scratch_shapes=[
            pltpu.SMEM(arrays[0].shape, jnp.int32),
            pltpu.SMEM(arrays[1].shape, jnp.int32),
            pltpu.SemaphoreType.DMA((slots + 3,)),
        ],
        compiler_params=room,
        name="prepare",
    )(*[x if i == 1 else pltpu.with_memory_space_constraint(x, pltpu.HBM) for i, x in enumerate(arrays)])


def partial_kernel(guide, samples, diag, high, low, *refs):
    pieces = refs[:-4]
    groups = 2 * len(pieces)
    kept, sent, panel, total = refs[-4:]
    col = lax.axis_index("col")
    rep = lax.axis_index("rep")
    rows = samples.shape[1]
    for turn, piece in enumerate(pieces):
        for half in range(2):
            block = guide[2, turn] ^ half
            panel[block, :rows], panel[block, rows:] = halves(piece[half])
    total[...] = jnp.zeros_like(total)

    def term(x_high, both, w_high, w_low):
        wide = dot(both, w_high)
        return wide[:rows] + wide[rows:] + dot(x_high, w_low)

    own_high, own_low = halves(samples[0])
    total[col * 2 + rep] = term(
        own_high, jnp.concatenate([own_high, own_low], axis=0), *halves(diag[0])
    )
    for slot in range(high.shape[0]):
        source = panel.at[guide[1, slot]]
        value = term(source[:rows], source[...], high[slot], low[slot])
        total[guide[0, slot]] += jnp.where(slot < guide[4, 0], value, 0.0)
    for pair in range(groups // 2):
        kept[pair] = total[2 * pair + rep]
        sent[pair] = total[2 * pair + 1 - rep]


def partial_image(guide, samples, diag, high, low, pieces):
    groups = 2 * len(pieces)
    _, rows, side = samples.shape
    half = jax.ShapeDtypeStruct((groups // 2, rows, side), f32)
    panel = jax.ShapeDtypeStruct((groups, 2 * rows, side), bf16)
    return pl.pallas_call(
        partial_kernel,
        out_shape=(half, half, panel),
        in_specs=[smem] + [vmem] * (4 + len(pieces)),
        out_specs=(vmem, vmem, vmem),
        scratch_shapes=[pltpu.VMEM((groups, rows, side), f32)],
        compiler_params=room,
        name="partial_image",
    )(guide, samples, diag, high, low, *pieces)


def half_gradient_kernel(
    guide, own_image, other_image, samples, panel, diag, tiles, moved, new_diag, wide, low, step, sem
):
    pairs, rows, side = own_image.shape
    rep = lax.axis_index("rep")
    left_high, left_low = halves(samples[0].T)
    right_high, right_low = halves(own_image[lax.axis_index("col")])
    one_side = dot(left_high, right_high) + dot(left_low, right_high) + dot(left_high, right_low)
    tile = diag[0]
    line = lax.broadcasted_iota(jnp.int32, (side, side), 0)
    on_diag = line == lax.broadcasted_iota(jnp.int32, (side, side), 1)
    scale = step_size / (2.0 * rows)
    shifted = tile - (one_side + one_side.T) * scale
    inverse = step_size / jnp.where(on_diag, tile, 1.0)
    step[0] = jnp.where(on_diag, shifted + inverse, soft_limit(shifted))
    copy = pltpu.make_async_copy(step, new_diag, sem)
    copy.start()
    for pair in range(pairs):
        for parity, image in ((rep, own_image), (1 - rep, other_image)):
            block = 2 * pair + parity
            image_high, low[block] = halves(image[pair].T)
            wide[block, :, :rows] = image_high
            wide[block, :, rows:] = image_high
    for slot in range(tiles.shape[0]):
        left, right = guide[0, slot], guide[1, slot]
        gradient = dot(wide[left], panel[right]) + dot(low[left], panel[right, :rows])
        moved[slot] = tiles[slot] - gradient * scale
    copy.wait()


def half_gradient(guide, own_image, other_image, samples, panel, diag, tiles):
    groups, _, side = panel.shape
    rows = samples.shape[1]
    return pl.pallas_call(
        half_gradient_kernel,
        out_shape=(
            jax.ShapeDtypeStruct(tiles.shape, f32),
            jax.ShapeDtypeStruct(diag.shape, f32),
        ),
        in_specs=[smem] + [vmem] * 6,
        out_specs=(vmem, hbm),
        scratch_shapes=[
            pltpu.VMEM((groups, side, 2 * rows), bf16),
            pltpu.VMEM((groups, side, rows), bf16),
            pltpu.VMEM(diag.shape, f32),
            pltpu.SemaphoreType.DMA,
        ],
        compiler_params=room,
        name="half_gradient",
    )(guide, own_image, other_image, samples, panel, diag, tiles)


def row_panel_kernel(pair, *refs):
    pieces, (wide, low) = refs[:-2], refs[-2:]
    rep = lax.axis_index("rep")
    col = lax.axis_index("col")
    pairs, rows = len(pieces) // 2 + 1, pair.shape[1]
    lines = [(pair[0], pair[1])]
    lines += [(pieces[k][...], pieces[k + pairs - 1][...]) for k in range(pairs - 1)]
    for turn, (same, other) in enumerate(lines):
        line = 2 * lax.rem(col + pairs - turn, pairs)
        for block, values in ((line + rep, same), (line + 1 - rep, other)):
            high, low[block] = halves(values.T)
            wide[block, :, :rows] = high
            wide[block, :, rows:] = high


def row_panel(pair, pieces):
    _, rows, side = pair.shape
    groups = len(pieces) + 2
    return pl.pallas_call(
        row_panel_kernel,
        out_shape=(
            jax.ShapeDtypeStruct((groups, side, 2 * rows), bf16),
            jax.ShapeDtypeStruct((groups, side, rows), bf16),
        ),
        in_specs=[vmem] * (1 + len(pieces)),
        out_specs=(vmem, vmem),
        compiler_params=room,
        name="row_panel",
    )(pair, *pieces)


def slots_kernel(turn, guide, wide, low, piece, moved, *refs):
    out, panel, ready, sems = refs[-4:]
    pairs, rows, _ = piece.shape
    for pair in range(pairs):
        panel[pair, :rows], panel[pair, rows:] = halves(piece[pair])
    parity = guide[3, turn]
    copies = [
        pltpu.make_async_copy(ready.at[slot], out.at[slot], sems.at[slot])
        for slot in range(moved.shape[0])
    ]
    for slot, copy in enumerate(copies):
        left, right = guide[0, slot], lax.div(guide[1, slot], 2)
        gradient = dot(wide[left], panel[right]) + dot(low[left], panel[right, :rows])
        value = soft_limit(moved[slot] - gradient * (step_size / (2.0 * rows)))
        ready[slot] = jnp.where(slot < guide[4, 0], value, 0.0)
        pl.when(guide[1, slot] & 1 == parity)(copy.start)
    for slot, copy in enumerate(copies):
        pl.when(guide[1, slot] & 1 == parity)(copy.wait)


def update_slots(turn, guide, wide, low, piece, moved, *begun):
    slots, side, _ = moved.shape
    groups, _, depth = wide.shape
    return pl.pallas_call(
        functools.partial(slots_kernel, turn),
        out_shape=jax.ShapeDtypeStruct(moved.shape, f32),
        in_specs=[smem] + [vmem] * 4 + [hbm] * len(begun),
        out_specs=hbm,
        input_output_aliases={5: 0} if begun else {},
        scratch_shapes=[
            pltpu.VMEM((groups // 2, depth, side), bf16),
            pltpu.VMEM(moved.shape, f32),
            pltpu.SemaphoreType.DMA((slots,)),
        ],
        compiler_params=room,
        name="update_slots",
    )(guide, wide, low, piece, moved, *begun)


def on_device(samples, diag_tiles, omega_slots, tile_pos, tile_count):
    groups = lax.axis_size(line_axes)
    cols = lax.axis_size("col")
    slots, side = omega_slots.shape[2], omega_slots.shape[3]
    tiles = omega_slots.reshape(slots, side, side)
    place = tile_pos.reshape(slots, 2).T
    span = range(groups)

    def links(source, turn):
        return [
            (line * groups + source(turn, row, line, groups), row * groups + line)
            for line in span
            for row in span
        ]

    def around(size, turn):
        return [(j, (j + turn) % size) for j in range(size)]

    first = samples[None]
    pair = lax.dynamic_update_slice(jnp.zeros((2, *samples.shape), f32), first, (0, 0, 0))
    pair = lax.optimization_barrier(pair)
    pair = lax.dynamic_update_slice(
        pair, lax.ppermute(first, "rep", around(2, 1)), (1, 0, 0)
    )
    col_pieces = [
        lax.ppermute(pair, grid_axes, links(sample_source, turn)) for turn in range(cols)
    ]
    guide, own_diag, held, high, low = prepare(groups, place, tile_count, diag_tiles, tiles)
    kept, sent, panel = partial_image(guide, pair, own_diag, high, low, col_pieces)
    chip = kept + lax.ppermute(sent, "rep", around(2, 1))
    image = chip
    for turn in range(1, cols):
        image = image + lax.ppermute(chip, "col", around(cols, turn))

    samples_late, image = lax.optimization_barrier((samples, image))
    beside = [lax.ppermute(samples_late, "col", around(cols, turn)) for turn in range(1, cols)]
    across = [lax.ppermute(block, "rep", around(2, 1)) for block in beside]
    first, second = [
        lax.ppermute(image, grid_axes, links(image_source, turn)) for turn in range(2)
    ]
    other = lax.ppermute(image, "rep", around(2, 1))
    moved, new_diag = half_gradient(guide, image, other, pair, panel, own_diag, held)
    beside, moved = lax.optimization_barrier((beside + across, moved))
    wide, low = row_panel(pair, beside)
    begun = update_slots(0, guide, wide, low, first, moved)
    new_slots = update_slots(1, guide, wide, low, second, moved, begun)
    return new_slots.reshape(omega_slots.shape), new_diag


def solution(mesh):
    placed = (
        P("parts", ("row", "col", "rep")),
        P(("parts", "row", "col", "rep"), None, None),
        P(("parts", "row"), ("col", "rep"), None, None, None),
        P(("parts", "row"), ("col", "rep"), None, None),
        P(("parts", "row"), ("col", "rep")),
    )
    return jax.shard_map(
        on_device,
        mesh=mesh,
        in_specs=placed,
        out_specs=(
            P(("parts", "row"), ("col", "rep"), None, None, None),
            P(("parts", "row", "col", "rep"), None, None),
        ),
        check_vma=False,
    )
```

```python
import functools

import jax
import jax.numpy as jnp
from jax import lax
from jax.experimental import pallas as pl
from jax.experimental.pallas import tpu as pltpu
from jax.sharding import PartitionSpec as P

step_size = 1.0
penalty = 0.1
grid_axes = ("row", "col", "rep")
line_axes = ("col", "rep")
f32 = jnp.float32
bf16 = jnp.bfloat16
vmem = pl.BlockSpec(memory_space=pltpu.VMEM)
smem = pl.BlockSpec(memory_space=pltpu.SMEM)
hbm = pl.BlockSpec(memory_space=pltpu.HBM)
room = pltpu.CompilerParams(vmem_limit_bytes=24 * 2**20)


def halves(values):
    high = values.astype(bf16)
    return high, (values - high.astype(f32)).astype(bf16)


def dot(left, right):
    return jnp.dot(left, right, preferred_element_type=f32)


def soft_limit(values):
    limit_value = step_size * penalty
    return values - jnp.clip(values, -limit_value, limit_value)


def first_source(row, own, groups):
    rep = (row // 2 ^ row ^ own // (groups // 2)) & 1
    return 2 * (row // 2 ^ rep) + rep


def sample_source(turn, row, own, groups):
    return first_source(row, own, groups) ^ (2 * turn + turn % 2)


def image_source(turn, row, own, groups):
    return first_source(row, own, groups) ^ ((1 - turn) * (groups - 1))


def prepare_kernel(groups, *refs):
    place, count, *arrays = refs[:4]
    guide, *held, high, low, spots, live, sems = refs[4:]
    tiles = held[1]
    slots = tiles.shape[0]
    pairs = [(place, spots), (count, live), (arrays[0], held[0])]
    pairs += [(arrays[1].at[slot], tiles.at[slot]) for slot in range(slots)]
    copies = [pltpu.make_async_copy(*pair, sems.at[i]) for i, pair in enumerate(pairs)]
    for copy in copies:
        copy.start()
    row = lax.axis_index("row")
    own = lax.axis_index("col") * 2 + lax.axis_index("rep")
    for turn in range(groups // 2):
        guide[2, turn] = sample_source(turn, row, own, groups)
    for turn in range(2):
        guide[3, turn] = image_source(turn, row, own, groups) & 1
    for slot in range(slots):
        copies[3 + slot].wait()
        high[slot], low[slot] = halves(tiles[slot].T)
    for copy in copies[:3]:
        copy.wait()
    for slot in range(slots):
        guide[0, slot] = spots[0, slot]
        guide[1, slot] = spots[1, slot]
    guide[4, 0] = live[0, 0]


def prepare(groups, *arrays):
    slots = arrays[-1].shape[0]
    width = max(slots, groups)
    held = [jax.ShapeDtypeStruct(x.shape, x.dtype) for x in arrays[2:]]
    half = jax.ShapeDtypeStruct(arrays[-1].shape, bf16)
    return pl.pallas_call(
        functools.partial(prepare_kernel, groups),
        out_shape=(pltpu.SMEM((5, width), jnp.int32), *held, half, half),
        in_specs=[hbm, vmem, hbm, hbm],
        out_specs=(smem,) + (vmem,) * 4,
        scratch_shapes=[
            pltpu.SMEM(arrays[0].shape, jnp.int32),
            pltpu.SMEM(arrays[1].shape, jnp.int32),
            pltpu.SemaphoreType.DMA((slots + 3,)),
        ],
        compiler_params=room,
        name="prepare",
    )(*[x if i == 1 else pltpu.with_memory_space_constraint(x, pltpu.HBM) for i, x in enumerate(arrays)])


def partial_kernel(guide, samples, diag, high, low, *refs):
    pieces = refs[:-4]
    groups = 2 * len(pieces)
    kept, sent, panel, total = refs[-4:]
    col = lax.axis_index("col")
    rep = lax.axis_index("rep")
    rows = samples.shape[1]
    for turn, piece in enumerate(pieces):
        for half in range(2):
            block = guide[2, turn] ^ half
            panel[block, :rows], panel[block, rows:] = halves(piece[half])
    total[...] = jnp.zeros_like(total)

    def term(x_high, both, w_high, w_low):
        wide = dot(both, w_high)
        return wide[:rows] + wide[rows:] + dot(x_high, w_low)

    own_high, own_low = halves(samples[0])
    total[col * 2 + rep] = term(
        own_high, jnp.concatenate([own_high, own_low], axis=0), *halves(diag[0])
    )
    for slot in range(high.shape[0]):
        source = panel.at[guide[1, slot]]
        value = term(source[:rows], source[...], high[slot], low[slot])
        total[guide[0, slot]] += jnp.where(slot < guide[4, 0], value, 0.0)
    for pair in range(groups // 2):
        kept[pair] = total[2 * pair + rep]
        sent[pair] = total[2 * pair + 1 - rep]


def partial_image(guide, samples, diag, high, low, pieces):
    groups = 2 * len(pieces)
    _, rows, side = samples.shape
    half = jax.ShapeDtypeStruct((groups // 2, rows, side), f32)
    panel = jax.ShapeDtypeStruct((groups, 2 * rows, side), bf16)
    return pl.pallas_call(
        partial_kernel,
        out_shape=(half, half, panel),
        in_specs=[smem] + [vmem] * (4 + len(pieces)),
        out_specs=(vmem, vmem, vmem),
        scratch_shapes=[pltpu.VMEM((groups, rows, side), f32)],
        compiler_params=room,
        name="partial_image",
    )(guide, samples, diag, high, low, *pieces)


def half_gradient_kernel(
    guide, own_image, other_image, samples, panel, diag, tiles, moved, new_diag, wide, low, step, sem
):
    pairs, rows, side = own_image.shape
    rep = lax.axis_index("rep")
    left_high, left_low = halves(samples[0].T)
    right_high, right_low = halves(own_image[lax.axis_index("col")])
    one_side = dot(left_high, right_high) + dot(left_low, right_high) + dot(left_high, right_low)
    tile = diag[0]
    line = lax.broadcasted_iota(jnp.int32, (side, side), 0)
    on_diag = line == lax.broadcasted_iota(jnp.int32, (side, side), 1)
    scale = step_size / (2.0 * rows)
    shifted = tile - (one_side + one_side.T) * scale
    inverse = step_size / jnp.where(on_diag, tile, 1.0)
    step[0] = jnp.where(on_diag, shifted + inverse, soft_limit(shifted))
    copy = pltpu.make_async_copy(step, new_diag, sem)
    copy.start()
    for pair in range(pairs):
        for parity, image in ((rep, own_image), (1 - rep, other_image)):
            block = 2 * pair + parity
            image_high, low[block] = halves(image[pair].T)
            wide[block, :, :rows] = image_high
            wide[block, :, rows:] = image_high
    for slot in range(tiles.shape[0]):
        left, right = guide[0, slot], guide[1, slot]
        gradient = dot(wide[left], panel[right]) + dot(low[left], panel[right, :rows])
        moved[slot] = tiles[slot] - gradient * scale
    copy.wait()


def half_gradient(guide, own_image, other_image, samples, panel, diag, tiles):
    groups, _, side = panel.shape
    rows = samples.shape[1]
    return pl.pallas_call(
        half_gradient_kernel,
        out_shape=(
            jax.ShapeDtypeStruct(tiles.shape, f32),
            jax.ShapeDtypeStruct(diag.shape, f32),
        ),
        in_specs=[smem] + [vmem] * 6,
        out_specs=(vmem, hbm),
        scratch_shapes=[
            pltpu.VMEM((groups, side, 2 * rows), bf16),
            pltpu.VMEM((groups, side, rows), bf16),
            pltpu.VMEM(diag.shape, f32),
            pltpu.SemaphoreType.DMA,
        ],
        compiler_params=room,
        name="half_gradient",
    )(guide, own_image, other_image, samples, panel, diag, tiles)


def row_panel_kernel(pair, *refs):
    pieces, (wide, low) = refs[:-2], refs[-2:]
    rep = lax.axis_index("rep")
    col = lax.axis_index("col")
    pairs, rows = len(pieces) // 2 + 1, pair.shape[1]
    lines = [(pair[0], pair[1])]
    lines += [(pieces[k][...], pieces[k + pairs - 1][...]) for k in range(pairs - 1)]
    for turn, (same, other) in enumerate(lines):
        line = 2 * lax.rem(col + pairs - turn, pairs)
        for block, values in ((line + rep, same), (line + 1 - rep, other)):
            high, low[block] = halves(values.T * (step_size / (2.0 * rows)))
            wide[block, :, :rows] = high
            wide[block, :, rows:] = high


def row_panel(pair, pieces):
    _, rows, side = pair.shape
    groups = len(pieces) + 2
    return pl.pallas_call(
        row_panel_kernel,
        out_shape=(
            jax.ShapeDtypeStruct((groups, side, 2 * rows), bf16),
            jax.ShapeDtypeStruct((groups, side, rows), bf16),
        ),
        in_specs=[vmem] * (1 + len(pieces)),
        out_specs=(vmem, vmem),
        compiler_params=room,
        name="row_panel",
    )(pair, *pieces)


def slots_kernel(turn, guide, wide, low, piece, moved, *refs):
    out, panel, ready, sems = refs[-4:]
    pairs, rows, _ = piece.shape
    for pair in range(pairs):
        panel[pair, :rows], panel[pair, rows:] = halves(piece[pair])
    parity = guide[3, turn]
    copies = [
        pltpu.make_async_copy(ready.at[slot], out.at[slot], sems.at[slot])
        for slot in range(moved.shape[0])
    ]
    for slot, copy in enumerate(copies):
        left, right = guide[0, slot], lax.div(guide[1, slot], 2)
        gradient = dot(wide[left], panel[right]) + dot(low[left], panel[right, :rows])
        value = soft_limit(moved[slot] - gradient)
        ready[slot] = jnp.where(slot < guide[4, 0], value, 0.0)
        pl.when(guide[1, slot] & 1 == parity)(copy.start)
    for slot, copy in enumerate(copies):
        pl.when(guide[1, slot] & 1 == parity)(copy.wait)


def update_slots(turn, guide, wide, low, piece, moved, *begun):
    slots, side, _ = moved.shape
    groups, _, depth = wide.shape
    return pl.pallas_call(
        functools.partial(slots_kernel, turn),
        out_shape=jax.ShapeDtypeStruct(moved.shape, f32),
        in_specs=[smem] + [vmem] * 4 + [hbm] * len(begun),
        out_specs=hbm,
        input_output_aliases={5: 0} if begun else {},
        scratch_shapes=[
            pltpu.VMEM((groups // 2, depth, side), bf16),
            pltpu.VMEM(moved.shape, f32),
            pltpu.SemaphoreType.DMA((slots,)),
        ],
        compiler_params=room,
        name="update_slots",
    )(guide, wide, low, piece, moved, *begun)


def on_device(samples, diag_tiles, omega_slots, tile_pos, tile_count):
    groups = lax.axis_size(line_axes)
    cols = lax.axis_size("col")
    slots, side = omega_slots.shape[2], omega_slots.shape[3]
    tiles = omega_slots.reshape(slots, side, side)
    place = tile_pos.reshape(slots, 2).T
    span = range(groups)

    def links(source, turn):
        return [
            (line * groups + source(turn, row, line, groups), row * groups + line)
            for line in span
            for row in span
        ]

    def around(size, turn):
        return [(j, (j + turn) % size) for j in range(size)]

    first = samples[None]
    pair = lax.dynamic_update_slice(jnp.zeros((2, *samples.shape), f32), first, (0, 0, 0))
    pair = lax.optimization_barrier(pair)
    pair = lax.dynamic_update_slice(
        pair, lax.ppermute(first, "rep", around(2, 1)), (1, 0, 0)
    )
    col_pieces = [
        lax.ppermute(pair, grid_axes, links(sample_source, turn)) for turn in range(cols)
    ]
    guide, own_diag, held, high, low = prepare(groups, place, tile_count, diag_tiles, tiles)
    kept, sent, panel = partial_image(guide, pair, own_diag, high, low, col_pieces)
    chip = kept + lax.ppermute(sent, "rep", around(2, 1))
    image = chip
    for turn in range(1, cols):
        image = image + lax.ppermute(chip, "col", around(cols, turn))

    samples_late, image = lax.optimization_barrier((samples, image))
    beside = [lax.ppermute(samples_late, "col", around(cols, turn)) for turn in range(1, cols)]
    across = [lax.ppermute(block, "rep", around(2, 1)) for block in beside]
    first, second = [
        lax.ppermute(image, grid_axes, links(image_source, turn)) for turn in range(2)
    ]
    other = lax.ppermute(image, "rep", around(2, 1))
    moved, new_diag = half_gradient(guide, image, other, pair, panel, own_diag, held)
    beside, moved = lax.optimization_barrier((beside + across, moved))
    wide, low = row_panel(pair, beside)
    begun = update_slots(0, guide, wide, low, first, moved)
    new_slots = update_slots(1, guide, wide, low, second, moved, begun)
    return new_slots.reshape(omega_slots.shape), new_diag


def solution(mesh):
    placed = (
        P("parts", ("row", "col", "rep")),
        P(("parts", "row", "col", "rep"), None, None),
        P(("parts", "row"), ("col", "rep"), None, None, None),
        P(("parts", "row"), ("col", "rep"), None, None),
        P(("parts", "row"), ("col", "rep")),
    )
    return jax.shard_map(
        on_device,
        mesh=mesh,
        in_specs=placed,
        out_specs=(
            P(("parts", "row"), ("col", "rep"), None, None, None),
            P(("parts", "row", "col", "rep"), None, None),
        ),
        check_vma=False,
    )
```
